512 devices in a mesh: ctx: 128 (over y_hi, z, x), grp: 4 (over y_lo, core).
Axes of the slice: x: 4, y: 4 (y_hi: 2, y_lo: 2; y = y_hi * 2 + y_lo), z: 16, core: 2. Of those that a mesh axis runs over, the one named last changes fastest.
Arguments:
- query_branch: bfloat16 [256, 16384], P('grp', 'ctx'), may hold values from -6 to 6
- key_branch: bfloat16 [256, 16384], P('grp', 'ctx'), may hold values from -6 to 6
- value_branch: bfloat16 [256, 16384], P('grp', 'ctx'), may hold values from -6 to 6
- query_taps: float32 [256, 3], P('grp'), may hold values from -3.5 to 3.5
- key_taps: float32 [256, 3], P('grp'), may hold values from -3.5 to 3.5
- value_taps: float32 [256, 3], P('grp'), may hold values from -3.5 to 3.5
- long_filter: float32 [16384], P('ctx'), may hold values from -4 to 4
- grad_out: bfloat16 [256, 16384], P('grp', 'ctx'), may hold values from -1.5 to 1.5
Outputs:
- grad_query: float32 [256, 16384], P('grp', 'ctx')
- grad_key: float32 [256, 16384], P('grp', 'ctx')
- grad_value: float32 [256, 16384], P('grp', 'ctx')
- grad_filter: float32 [16384], P('ctx')
The draws below stay inside these ranges and needn't reach their ends.
All inputs are finite; a program needn't handle non-finite values.
Results may differ from the reference program's by a relative error of at most 0.00055.
Values may be sent and summed in bfloat16 or wider, within the bound.
A program may use at most 64 MiB of HBM per device.

```python
import math
import jax
import jax.numpy as jnp
from jax import lax

C = 256
TAPS = 3
LENGTH = 16384


def draw_long_filter(key, part):
    key = jax.random.fold_in(key, 11)
    return jnp.clip(jax.random.normal(key, (LENGTH,), jnp.float32), -4.0, 4.0)


def block_levels(key, dims, shards, smallest, largest):
    level = 1.0
    for dim, blocks in shards:
        draws = jax.random.uniform(jax.random.fold_in(jax.random.fold_in(key, 6), dim), (blocks,), jnp.float32, smallest / len(shards), largest / len(shards))
        level = level * jnp.repeat(jnp.exp(draws), dims[dim] // blocks).reshape((-1,) + (1,) * (len(dims) - 1 - dim))
    return level


def centred(own_key, shape, scale, most, shards=(), kind=jnp.bfloat16):
    level = block_levels(own_key, shape, shards, -0.22, 0.18) if shards else 1.0
    values = jax.random.normal(own_key, shape, jnp.float32) * scale * level
    return jnp.minimum(jnp.maximum(values, -most), most).astype(kind)


def setup_inputs(seed: int = 0) -> dict:
    keys = jax.random.split(jax.random.key(seed), 9)
    return {
        "query_branch": centred(keys[0], (C, LENGTH), 1.0, 6.0, ((0, 4), (1, 128))),
        "key_branch": centred(keys[1], (C, LENGTH), 1.0, 6.0, ((0, 4), (1, 128))),
        "value_branch": centred(keys[2], (C, LENGTH), 1.0, 6.0, ((0, 4), (1, 128))),
        "query_taps": centred(keys[3], (C, TAPS), TAPS ** -0.5, 3.5, ((0, 4),), jnp.float32),
        "key_taps": centred(keys[4], (C, TAPS), TAPS ** -0.5, 3.5, ((0, 4),), jnp.float32),
        "value_taps": centred(keys[5], (C, TAPS), TAPS ** -0.5, 3.5, ((0, 4),), jnp.float32),
        "long_filter": draw_long_filter(jax.random.fold_in(keys[8], 71), 0),
        "grad_out": centred(keys[7], (C, LENGTH), 0.25, 1.5, ((0, 4), (1, 128))),
    }


def conv_taps(branch, taps):
    signal = branch.astype(jnp.float32)
    count = signal.shape[1]
    padded = jnp.pad(signal, ((0, 0), (2, 0)))
    return taps[:, 0:1] * padded[:, 2:] + taps[:, 1:2] * padded[:, 1:count + 1] + taps[:, 2:3] * padded[:, 0:count]

def conv_back(gradient, taps):
    count = gradient.shape[1]
    padded = jnp.pad(gradient, ((0, 0), (0, 2)))
    return taps[:, 0:1] * padded[:, 0:count] + taps[:, 1:2] * padded[:, 1:count + 1] + taps[:, 2:3] * padded[:, 2:]

def reference(query_branch, key_branch, value_branch, query_taps, key_taps, value_taps, long_filter, grad_out):
    query_conv = conv_taps(query_branch, query_taps)
    key_conv = conv_taps(key_branch, key_taps)
    value_conv = conv_taps(value_branch, value_taps)
    gated = key_conv * value_conv
    grad_long = grad_out.astype(jnp.float32) * query_conv
    padded_len = 2 * LENGTH
    scale_factor = 1.0 / math.sqrt(LENGTH)
    spec_gated = jnp.fft.rfft(gated, n=padded_len, axis=1)
    spec_filter = jnp.fft.rfft(long_filter, n=padded_len)
    spec_grad = jnp.fft.rfft(grad_long, n=padded_len, axis=1)
    long_out = jnp.fft.irfft(spec_gated * spec_filter[None, :], n=padded_len, axis=1)[:, :LENGTH] * scale_factor
    grad_gated = jnp.fft.irfft(spec_grad * jnp.conj(spec_filter)[None, :], n=padded_len, axis=1)[:, :LENGTH] * scale_factor
    cross_spec = lax.optimization_barrier(jnp.sum(spec_grad * jnp.conj(spec_gated), axis=0))
    grad_filter = jnp.fft.irfft(cross_spec, n=padded_len)[:LENGTH] * scale_factor
    grad_qconv = grad_out.astype(jnp.float32) * long_out
    grad_kconv = grad_gated * value_conv
    grad_vconv = grad_gated * key_conv
    grad_query = conv_back(grad_qconv, query_taps)
    grad_key = conv_back(grad_kconv, key_taps)
    grad_value = conv_back(grad_vconv, value_taps)
    return (grad_query, grad_key, grad_value, grad_filter)
```

```python
import functools
import math

import jax
import jax.numpy as jnp
import ml_dtypes
import numpy as np
from jax import lax
from jax.experimental import pallas as pl
from jax.experimental.pallas import tpu as pltpu
from jax.sharding import PartitionSpec as P

NY, NZ, NX, NG = 2, 16, 4, 4
NP = NY * NX
NI = NP // 2
BLK = 128
NB = NY * NZ * NX
FULL = 2 * BLK * NB
MESH = pl.DeviceIdType.MESH
Z_STEPS = (8, 7, 9, 6, 10, 5, 11, 4, 12, 3, 13, 2, 14, 1, 15)
F32, BF16 = jnp.float32, jnp.bfloat16


def split_np(matrix):
    high = matrix.astype(np.float32).astype(ml_dtypes.bfloat16)
    low = (matrix - high.astype(np.float64)).astype(np.float32).astype(ml_dtypes.bfloat16)
    return np.stack([high, low])


@functools.lru_cache(maxsize=None)
def tables():
    half = np.arange(NB) + 0.5
    blocks = np.arange(NB)
    pos = np.arange(BLK)
    outer = 2.0 * np.pi * half[:, None] * blocks[None, :] / (2 * NB)
    fwd_outer = np.concatenate([np.cos(outer), -np.sin(outer)], axis=0)
    twist = 2.0 * np.pi * half[:, None] * pos[None, :] / FULL
    twists = np.stack([np.cos(twist), np.sin(twist)]).astype(np.float32)
    inner = 2.0 * np.pi * ((pos[:, None] * pos[None, :]) % BLK) / BLK
    cos, sin = np.cos(inner), np.sin(inner)
    fwd_inner = np.block([[cos, -sin], [sin, cos]])
    scale = 2.0 / (FULL * math.sqrt(BLK * NB))
    inv_outer = scale * np.concatenate([np.cos(outer).T, -np.sin(outer).T], axis=1)
    return (
        split_np(fwd_outer),
        twists,
        split_np(fwd_inner),
        split_np(fwd_inner.T.copy()),
        split_np(inv_outer),
    )


def split(value):
    high = value.astype(BF16)
    return high, (value - high.astype(F32)).astype(BF16)


def dot(left, right):
    return jnp.dot(left, right, preferred_element_type=F32)


def left_table(table, value):
    high, low = split(value)
    return dot(table[0], high) + (dot(table[0], low) + dot(table[1], high))


def right_table(value, table):
    high, low = split(value)
    return dot(high, table[0]) + (dot(low, table[0]) + dot(high, table[1]))


def earlier(value, steps):
    lane = lax.broadcasted_iota(jnp.int32, value.shape, 1)
    row = lax.broadcasted_iota(jnp.int32, value.shape, 0)
    turned = pltpu.roll(value, steps, 1)
    above = jnp.where(row == 0, 0.0, pltpu.roll(turned, 1, 0))
    return jnp.where(lane < steps, above, turned)


def later(value, steps):
    lane = lax.broadcasted_iota(jnp.int32, value.shape, 1)
    row = lax.broadcasted_iota(jnp.int32, value.shape, 0)
    turned = pltpu.roll(value, BLK - steps, 1)
    below = jnp.where(row == NB - 1, 0.0, pltpu.roll(turned, NB - 1, 0))
    return jnp.where(lane >= BLK - steps, below, turned)


def kernel(
    q_ref, k_ref, v_ref, g_ref, tq_ref, tk_ref, tv_ref, filt_ref,
    fo_hbm, tw_hbm, fi_hbm, ii_hbm, io_hbm,
    oq_ref, ok_ref, ov_ref, of_ref,
    fo, tw, fi, ii, io,
    stage, s1, r1, r1f, s2, r2, s2f, r2f, tok, res, s3, r3, s4, r4, s5, r5,
    const_sem, z_send, z_recv, zf_send, zf_recv, p_send, p_recv, pf_send, pf_recv,
    b_send, b_recv, c_send, c_recv, g_send, g_recv,
):
    me = lax.axis_index("ctx")
    grp = lax.axis_index("grp")
    y, z, x = me // (NZ * NX), (me // NX) % NZ, me % NX
    p = y * NX + x
    pair, role = p // 2, p % 2

    def z_peer(step):
        other = (z + step) % NZ
        return other, {"ctx": (y * NZ + other) * NX + x}

    def p_peer(step):
        other = (p + step) % NP
        return other, {"ctx": ((other // NX) * NZ + z) * NX + other % NX}

    def g_peer(step):
        return {"grp": (grp + step) % NG}

    barrier = pltpu.get_barrier_semaphore()
    for step in Z_STEPS:
        pl.semaphore_signal(barrier, inc=1, device_id=z_peer(step)[1], device_id_type=MESH)
    for step in range(1, NP):
        pl.semaphore_signal(barrier, inc=1, device_id=p_peer(step)[1], device_id_type=MESH)
    for step in range(1, NG):
        pl.semaphore_signal(barrier, inc=1, device_id=g_peer(step), device_id_type=MESH)

    loads = [
        pltpu.make_async_copy(src, dst, const_sem.at[n])
        for n, (src, dst) in enumerate(
            ((fo_hbm, fo), (tw_hbm, tw), (fi_hbm, fi), (ii_hbm, ii), (io_hbm, io))
        )
    ]
    for load in loads:
        load.start()

    sends = []

    def send(src, dst, send_sem, recv_sem, target):
        copy = pltpu.make_async_remote_copy(
            src_ref=src, dst_ref=dst, send_sem=send_sem, recv_sem=recv_sem,
            device_id=target, device_id_type=MESH,
        )
        copy.start()
        sends.append(copy)

    def arrived(ref, sem):
        pltpu.make_async_copy(ref, ref, sem).wait()

    channels = q_ref.shape[0]
    for n, ref in enumerate((q_ref, k_ref, v_ref, g_ref)):
        stage[n * channels : (n + 1) * channels, :] = ref[...].astype(F32)
    for other in range(NZ):
        s1[other] = stage[pl.ds(other, 16, stride=NZ), :].astype(BF16)
    pl.semaphore_wait(barrier, len(Z_STEPS) + NP - 1 + NG - 1)

    for n, step in enumerate(Z_STEPS):
        other, target = z_peer(step)
        send(s1.at[other], r1.at[z], z_send.at[n], z_recv, target)
    for n, step in enumerate(Z_STEPS):
        other, target = z_peer(step)
        send(filt_ref, r1f.at[z], zf_send.at[n], zf_recv, target)
    r1[z] = s1[z]
    r1f[z] = filt_ref[...]
    arrived(r1.at[pl.ds(0, NZ - 1)], z_recv)

    stage[...] = r1[...].astype(F32).reshape(NZ * 16, BLK)
    for i in range(NI):
        for n in range(4):
            s2[i, n] = stage[pl.ds(n * NI + i, NZ, stride=16), :].astype(BF16)
    for n, step in enumerate(range(1, NP)):
        other, target = p_peer(step)
        send(s2.at[other // 2], r2.at[p], p_send.at[n], p_recv, target)
    arrived(r1f.at[pl.ds(0, NZ - 1)], zf_recv)
    s2f[...] = r1f[...].reshape(NZ, BLK)
    for n, step in enumerate(range(1, NP)):
        other, target = p_peer(step)
        send(s2f, r2f.at[p], pf_send.at[n], pf_recv, target)
    r2[p] = s2[pair]
    r2f[p] = s2f[...]
    arrived(r2.at[pl.ds(0, NP - 1)], p_recv)

    def rows_of(other):
        return pl.ds((other // NX) * NZ * NX + other % NX, NZ, stride=NX)

    for other in range(NP):
        for n in range(4):
            tok[n, rows_of(other), :] = r2[other, n].astype(F32)
    arrived(r2f.at[pl.ds(0, NP - 1)], pf_recv)
    for other in range(NP):
        tok[4, rows_of(other), :] = r2f[other]

    channel = z + NZ * pair
    taps = [[ref[channel, j] for j in range(3)] for ref in (tq_ref, tk_ref, tv_ref)]

    def conv(value, weights):
        return weights[0] * value + weights[1] * earlier(value, 1) + weights[2] * earlier(value, 2)

    grad_out = tok[3]
    key_conv = conv(tok[1], taps[1])
    value_conv = conv(tok[2], taps[2])
    gated = key_conv * value_conv
    grad_long = grad_out * conv(tok[0], taps[0])

    for load in loads:
        load.wait()
    signals = jnp.concatenate([gated, grad_long, tok[4]], axis=1)
    outer = left_table(fo, signals)
    cos, sin = tw[0], tw[1]
    turned = []
    for n in range(3):
        re = outer[:NB, n * BLK : (n + 1) * BLK]
        im = outer[NB:, n * BLK : (n + 1) * BLK]
        turned.append(jnp.concatenate([re * cos + im * sin, im * cos - re * sin], axis=1))
    spectra = right_table(jnp.concatenate(turned, axis=0), fi)
    gated_re, gated_im = spectra[:NB, :BLK], spectra[:NB, BLK:]
    grad_re, grad_im = spectra[NB : 2 * NB, :BLK], spectra[NB : 2 * NB, BLK:]
    filt_re, filt_im = spectra[2 * NB :, :BLK], spectra[2 * NB :, BLK:]

    first = role == 0
    left_re = jnp.where(first, gated_re, grad_re)
    left_im = jnp.where(first, gated_im, grad_im)
    turn_im = jnp.where(first, filt_im, -filt_im)
    main = jnp.concatenate(
        [left_re * filt_re - left_im * turn_im, left_re * turn_im + left_im * filt_re], axis=1
    )
    cross = jnp.concatenate(
        [grad_re * gated_re + grad_im * gated_im, grad_im * gated_re - grad_re * gated_im], axis=1
    )
    inner = right_table(jnp.concatenate([main, cross], axis=0), ii)
    backs = []
    for n in range(2):
        re = inner[n * NB : (n + 1) * NB, :BLK]
        im = inner[n * NB : (n + 1) * NB, BLK:]
        backs.append(jnp.concatenate([re * cos - im * sin, im * cos + re * sin], axis=0))
    tokens = left_table(io, jnp.concatenate(backs, axis=1))
    main_tok, cross_tok = tokens[:, :BLK], tokens[:, BLK:]

    def back(value, weights):
        return weights[0] * value + weights[1] * later(value, 1) + weights[2] * later(value, 2)

    def chosen(mine, other):
        return [jnp.where(first, a, b) for a, b in zip(mine, other)]

    res[0] = back(
        main_tok * jnp.where(first, grad_out, value_conv), chosen(taps[0], taps[1])
    )
    res[1] = jnp.where(first, cross_tok, back(main_tok * key_conv, taps[2]))

    for other in range(NP):
        for n in range(2):
            s3[other, n] = res[n, rows_of(other), :]
    for n, step in enumerate(range(1, NP)):
        other, target = p_peer(step)
        send(s3.at[other], r3.at[p], b_send.at[n], b_recv, target)
    r3[p] = s3[p]
    arrived(r3.at[pl.ds(0, NP - 1)], b_recv)

    for i in range(NI):
        s4[pl.ds(i, NZ, stride=16), :] = r3[2 * i, 0]
        s4[pl.ds(NI + i, NZ, stride=16), :] = r3[2 * i + 1, 0]
        s4[pl.ds(2 * NI + i, NZ, stride=16), :] = r3[2 * i + 1, 1]
    s4[pl.ds(12, NZ, stride=16), :] = (r3[0, 1] + r3[2, 1]) + (r3[4, 1] + r3[6, 1])
    for other in range(3):
        s4[pl.ds(13 + other, NZ, stride=16), :] = jnp.zeros((NZ, BLK), F32)
    my_rows = pl.ds(pl.multiple_of(z * 16, 16), 16)
    for n, step in enumerate(Z_STEPS):
        other, target = z_peer(step)
        rows = pl.ds(pl.multiple_of(other * 16, 16), 16)
        send(s4.at[rows], r4.at[my_rows], c_send.at[n], c_recv, target)
    r4[my_rows, :] = s4[my_rows, :]
    arrived(r4.at[pl.ds(0, (NZ - 1) * 16)], c_recv)

    total = jnp.sum(r4[pl.ds(12, NZ, stride=16), :], axis=0, keepdims=True)
    s5[...] = total
    for n, step in enumerate(range(1, NG)):
        send(s5, r5.at[grp], g_send.at[n], g_recv, g_peer(step))
    r5[grp] = total
    for n, ref in enumerate((oq_ref, ok_ref, ov_ref)):
        for i in range(NI):
            ref[i * NZ : (i + 1) * NZ, :] = r4[pl.ds(n * NI + i, NZ, stride=16), :]
    arrived(r5.at[pl.ds(0, NG - 1)], g_recv)
    of_ref[...] = (r5[0] + r5[1]) + (r5[2] + r5[3])
    for copy in sends:
        copy.wait_send()


def local(query_branch, key_branch, value_branch, query_taps, key_taps, value_taps, long_filter, grad_out):
    channels, count = query_branch.shape
    vmem = pl.BlockSpec(memory_space=pltpu.VMEM)
    smem = pl.BlockSpec(memory_space=pltpu.SMEM)
    hbm = pl.BlockSpec(memory_space=pl.ANY)
    consts = [jnp.asarray(table) for table in tables()]
    token_out = jax.ShapeDtypeStruct((channels, count), F32)
    sems = pltpu.SemaphoreType.DMA
    outs = pl.pallas_call(
        kernel,
        out_shape=(token_out, token_out, token_out, jax.ShapeDtypeStruct((1, count), F32)),
        in_specs=[vmem] * 4 + [smem] * 3 + [vmem] + [hbm] * 5,
        out_specs=(vmem,) * 4,
        scratch_shapes=[pltpu.VMEM(c.shape, c.dtype) for c in consts]
        + [
            pltpu.VMEM((4 * channels, BLK), F32),
            pltpu.VMEM((NZ, 16, BLK), BF16),
            pltpu.VMEM((NZ, 16, BLK), BF16),
            pltpu.VMEM((NZ, 1, BLK), F32),
            pltpu.VMEM((NI, 4, NZ, BLK), BF16),
            pltpu.VMEM((NP, 4, NZ, BLK), BF16),
            pltpu.VMEM((NZ, BLK), F32),
            pltpu.VMEM((NP, NZ, BLK), F32),
            pltpu.VMEM((5, NB, BLK), F32),
            pltpu.VMEM((2, NB, BLK), F32),
            pltpu.VMEM((NP, 2, NZ, BLK), F32),
            pltpu.VMEM((NP, 2, NZ, BLK), F32),
            pltpu.VMEM((NZ * 16, BLK), F32),
            pltpu.VMEM((NZ * 16, BLK), F32),
            pltpu.VMEM((1, BLK), F32),
            pltpu.VMEM((NG, 1, BLK), F32),
            sems((5,)),
            sems((NZ - 1,)), sems(()), sems((NZ - 1,)), sems(()),
            sems((NP - 1,)), sems(()), sems((NP - 1,)), sems(()),
            sems((NP - 1,)), sems(()),
            sems((NZ - 1,)), sems(()),
            sems((NG - 1,)), sems(()),
        ],
        compiler_params=pltpu.CompilerParams(
            collective_id=0, has_side_effects=True, vmem_limit_bytes=32 * 1024 * 1024
        ),
    )(
        query_branch, key_branch, value_branch, grad_out,
        query_taps, key_taps, value_taps, long_filter.reshape(1, count), *consts,
    )
    return outs[0], outs[1], outs[2], outs[3].reshape(count)


def solution(mesh):
    tokens = P("grp", "ctx")
    taps = P("grp", None)
    return jax.shard_map(
        local,
        mesh=mesh,
        in_specs=(tokens, tokens, tokens, taps, taps, taps, P("ctx"), tokens),
        out_specs=(tokens, tokens, tokens, P("ctx")),
        check_vma=False,
    )
```

```python
import functools
import math

import jax
import jax.numpy as jnp
import ml_dtypes
import numpy as np
from jax import lax
from jax.experimental import pallas as pl
from jax.experimental.pallas import tpu as pltpu
from jax.sharding import PartitionSpec as P

NY, NZ, NX, NG = 2, 16, 4, 4
NP = NY * NX
NI = NP // 2
BLK = 128
NB = NY * NZ * NX
FULL = 2 * BLK * NB
MESH = pl.DeviceIdType.MESH
Z_STEPS = (8, 7, 9, 6, 10, 5, 11, 4, 12, 3, 13, 2, 14, 1, 15)
F32, BF16 = jnp.float32, jnp.bfloat16


def split_np(matrix):
    high = matrix.astype(np.float32).astype(ml_dtypes.bfloat16)
    low = (matrix - high.astype(np.float64)).astype(np.float32).astype(ml_dtypes.bfloat16)
    return np.stack([high, low])


@functools.lru_cache(maxsize=None)
def tables():
    half = np.arange(NB) + 0.5
    blocks = np.arange(NB)
    pos = np.arange(BLK)
    outer = 2.0 * np.pi * half[:, None] * blocks[None, :] / (2 * NB)
    fwd_outer = np.concatenate([np.cos(outer), -np.sin(outer)], axis=0)
    twist = 2.0 * np.pi * half[:, None] * pos[None, :] / FULL
    twists = np.stack([np.cos(twist), np.sin(twist)]).astype(np.float32)
    inner = 2.0 * np.pi * ((pos[:, None] * pos[None, :]) % BLK) / BLK
    cos, sin = np.cos(inner), np.sin(inner)
    fwd_inner = np.block([[cos, -sin], [sin, cos]])
    scale = 2.0 / (FULL * math.sqrt(BLK * NB))
    inv_outer = scale * np.concatenate([np.cos(outer).T, -np.sin(outer).T], axis=1)
    return (
        split_np(fwd_outer),
        twists,
        split_np(fwd_inner),
        split_np(fwd_inner.T.copy()),
        split_np(inv_outer),
    )


def split(value):
    high = value.astype(BF16)
    return high, (value - high.astype(F32)).astype(BF16)


def dot(left, right):
    return jnp.dot(left, right, preferred_element_type=F32)


def left_table(table, value):
    high, low = split(value)
    return dot(table[0], high) + (dot(table[0], low) + dot(table[1], high))


def right_table(value, table):
    high, low = split(value)
    return dot(high, table[0]) + (dot(low, table[0]) + dot(high, table[1]))


def earlier(value, steps):
    lane = lax.broadcasted_iota(jnp.int32, value.shape, 1)
    row = lax.broadcasted_iota(jnp.int32, value.shape, 0)
    turned = pltpu.roll(value, steps, 1)
    above = jnp.where(row == 0, 0.0, pltpu.roll(turned, 1, 0))
    return jnp.where(lane < steps, above, turned)


def later(value, steps):
    lane = lax.broadcasted_iota(jnp.int32, value.shape, 1)
    row = lax.broadcasted_iota(jnp.int32, value.shape, 0)
    turned = pltpu.roll(value, BLK - steps, 1)
    below = jnp.where(row == NB - 1, 0.0, pltpu.roll(turned, NB - 1, 0))
    return jnp.where(lane >= BLK - steps, below, turned)


def kernel(
    q_hbm, k_hbm, v_hbm, g_hbm, filt_hbm, tq_hbm, tk_hbm, tv_hbm,
    fo_hbm, tw_hbm, fi_hbm, ii_hbm, io_hbm,
    r4, of_ref,
    q_ref, k_ref, v_ref, g_ref, filt_ref, tq_ref, tk_ref, tv_ref,
    fo, tw, fi, ii, io,
    stage, s1, r1, r1f, s2, r2, s2f, r2f, tok, res, s3, r3, s4, s5, r5,
    load_sem, z_send, z_recv, zf_send, zf_recv, p_send, p_recv, pf_send, pf_recv,
    b_send, b_recv, c_send, c_recv, g_send, g_recv,
):
    me = lax.axis_index("ctx")
    grp = lax.axis_index("grp")
    y, z, x = me // (NZ * NX), (me // NX) % NZ, me % NX
    p = y * NX + x
    pair, role = p // 2, p % 2

    def z_peer(step):
        other = (z + step) % NZ
        return other, {"ctx": (y * NZ + other) * NX + x}

    def p_peer(step):
        other = (p + step) % NP
        return other, {"ctx": ((other // NX) * NZ + z) * NX + other % NX}

    def g_peer(step):
        return {"grp": (grp + step) % NG}

    loads = [
        pltpu.make_async_copy(src, dst, load_sem.at[n])
        for n, (src, dst) in enumerate(
            (
                (q_hbm, q_ref), (k_hbm, k_ref), (v_hbm, v_ref), (g_hbm, g_ref), (filt_hbm, filt_ref),
                (tq_hbm, tq_ref), (tk_hbm, tk_ref), (tv_hbm, tv_ref),
                (fo_hbm, fo), (tw_hbm, tw), (fi_hbm, fi), (ii_hbm, ii), (io_hbm, io),
            )
        )
    ]
    for load in loads[:5]:
        load.start()
    barrier = pltpu.get_barrier_semaphore()
    for step in Z_STEPS:
        pl.semaphore_signal(barrier, inc=1, device_id=z_peer(step)[1], device_id_type=MESH)
    for step in range(1, NP):
        pl.semaphore_signal(barrier, inc=1, device_id=p_peer(step)[1], device_id_type=MESH)
    for step in range(1, NG):
        pl.semaphore_signal(barrier, inc=1, device_id=g_peer(step), device_id_type=MESH)

    for load in loads[5:]:
        load.start()

    sends = []

    def send(src, dst, send_sem, recv_sem, target):
        copy = pltpu.make_async_remote_copy(
            src_ref=src, dst_ref=dst, send_sem=send_sem, recv_sem=recv_sem,
            device_id=target, device_id_type=MESH,
        )
        copy.start()
        sends.append(copy)

    def arrived(ref, sem):
        pltpu.make_async_copy(ref, ref, sem).wait()

    for load in loads[:5]:
        load.wait()
    channels = q_ref.shape[0]
    for n, ref in enumerate((q_ref, k_ref, v_ref, g_ref)):
        stage[n * channels : (n + 1) * channels, :] = ref[...].astype(F32)
    for other in range(NZ):
        s1[other] = stage[pl.ds(other, 16, stride=NZ), :].astype(BF16)
    pl.semaphore_wait(barrier, len(Z_STEPS) + NP - 1 + NG - 1)

    for n, step in enumerate(Z_STEPS):
        other, target = z_peer(step)
        send(s1.at[other], r1.at[z], z_send.at[n], z_recv, target)
    for n, step in enumerate(Z_STEPS):
        other, target = z_peer(step)
        send(filt_ref, r1f.at[z], zf_send.at[n], zf_recv, target)
    r1[z] = s1[z]
    r1f[z] = filt_ref[...]
    arrived(r1.at[pl.ds(0, NZ - 1)], z_recv)

    stage[...] = r1[...].astype(F32).reshape(NZ * 16, BLK)
    for i in range(NI):
        for n in range(4):
            s2[i, n] = stage[pl.ds(n * NI + i, NZ, stride=16), :].astype(BF16)
    for n, step in enumerate(range(1, NP)):
        other, target = p_peer(step)
        send(s2.at[other // 2], r2.at[p], p_send.at[n], p_recv, target)
    arrived(r1f.at[pl.ds(0, NZ - 1)], zf_recv)
    s2f[...] = r1f[...].reshape(NZ, BLK)
    for n, step in enumerate(range(1, NP)):
        other, target = p_peer(step)
        send(s2f, r2f.at[p], pf_send.at[n], pf_recv, target)
    r2[p] = s2[pair]
    r2f[p] = s2f[...]
    arrived(r2.at[pl.ds(0, NP - 1)], p_recv)

    def rows_of(other):
        return pl.ds((other // NX) * NZ * NX + other % NX, NZ, stride=NX)

    for other in range(NP):
        for n in range(4):
            tok[n, rows_of(other), :] = r2[other, n].astype(F32)
    arrived(r2f.at[pl.ds(0, NP - 1)], pf_recv)
    for other in range(NP):
        tok[4, rows_of(other), :] = r2f[other]

    channel = z + NZ * pair
    for load in loads[5:8]:
        load.wait()
    taps = [[ref[j, channel] for j in range(3)] for ref in (tq_ref, tk_ref, tv_ref)]

    def conv(value, weights):
        return weights[0] * value + weights[1] * earlier(value, 1) + weights[2] * earlier(value, 2)

    grad_out = tok[3]
    key_conv = conv(tok[1], taps[1])
    value_conv = conv(tok[2], taps[2])
    gated = key_conv * value_conv
    grad_long = grad_out * conv(tok[0], taps[0])

    for load in loads[8:]:
        load.wait()
    signals = jnp.concatenate([gated, grad_long, tok[4]], axis=1)
    outer = left_table(fo, signals)
    cos, sin = tw[0], tw[1]
    turned = []
    for n in range(3):
        re = outer[:NB, n * BLK : (n + 1) * BLK]
        im = outer[NB:, n * BLK : (n + 1) * BLK]
        turned.append(jnp.concatenate([re * cos + im * sin, im * cos - re * sin], axis=1))
    spectra = right_table(jnp.concatenate(turned, axis=0), fi)
    gated_re, gated_im = spectra[:NB, :BLK], spectra[:NB, BLK:]
    grad_re, grad_im = spectra[NB : 2 * NB, :BLK], spectra[NB : 2 * NB, BLK:]
    filt_re, filt_im = spectra[2 * NB :, :BLK], spectra[2 * NB :, BLK:]

    first = role == 0
    left_re = jnp.where(first, gated_re, grad_re)
    left_im = jnp.where(first, gated_im, grad_im)
    turn_im = jnp.where(first, filt_im, -filt_im)
    main = jnp.concatenate(
        [left_re * filt_re - left_im * turn_im, left_re * turn_im + left_im * filt_re], axis=1
    )
    cross = jnp.concatenate(
        [grad_re * gated_re + grad_im * gated_im, grad_im * gated_re - grad_re * gated_im], axis=1
    )
    inner = right_table(jnp.concatenate([main, cross], axis=0), ii)
    backs = []
    for n in range(2):
        re = inner[n * NB : (n + 1) * NB, :BLK]
        im = inner[n * NB : (n + 1) * NB, BLK:]
        backs.append(jnp.concatenate([re * cos - im * sin, im * cos + re * sin], axis=0))
    tokens = left_table(io, jnp.concatenate(backs, axis=1))
    main_tok, cross_tok = tokens[:, :BLK], tokens[:, BLK:]

    def back(value, weights):
        return weights[0] * value + weights[1] * later(value, 1) + weights[2] * later(value, 2)

    def chosen(mine, other):
        return [jnp.where(first, a, b) for a, b in zip(mine, other)]

    res[0] = back(
        main_tok * jnp.where(first, grad_out, value_conv), chosen(taps[0], taps[1])
    )
    res[1] = jnp.where(first, cross_tok, back(main_tok * key_conv, taps[2]))

    for other in range(NP):
        for n in range(2):
            s3[other, n] = res[n, rows_of(other), :]
    for n, step in enumerate(range(1, NP)):
        other, target = p_peer(step)
        send(s3.at[other], r3.at[p], b_send.at[n], b_recv, target)
    r3[p] = s3[p]
    arrived(r3.at[pl.ds(0, NP - 1)], b_recv)

    for i in range(NI):
        s4[pl.ds(i, NZ, stride=16), :] = r3[2 * i, 0]
        s4[pl.ds(NI + i, NZ, stride=16), :] = r3[2 * i + 1, 0]
        s4[pl.ds(2 * NI + i, NZ, stride=16), :] = r3[2 * i + 1, 1]
    s4[pl.ds(12, NZ, stride=16), :] = (r3[0, 1] + r3[2, 1]) + (r3[4, 1] + r3[6, 1])
    my_rows = pl.ds(pl.multiple_of(z * 16, 16), 13)
    for n, step in enumerate(Z_STEPS):
        other, target = z_peer(step)
        rows = pl.ds(pl.multiple_of(other * 16, 16), 13)
        send(s4.at[rows], r4.at[my_rows], c_send.at[n], c_recv, target)
    r4[my_rows, :] = s4[my_rows, :]
    arrived(r4.at[pl.ds(0, (NZ - 1) * 13)], c_recv)

    total = jnp.sum(r4[pl.ds(12, NZ, stride=16), :], axis=0, keepdims=True)
    s5[...] = total
    for n, step in enumerate(range(1, NG)):
        send(s5, r5.at[grp], g_send.at[n], g_recv, g_peer(step))
    r5[grp] = total
    arrived(r5.at[pl.ds(0, NG - 1)], g_recv)
    of_ref[...] = (r5[0] + r5[1]) + (r5[2] + r5[3])
    for copy in sends:
        copy.wait_send()


def unpack(r4, total, oq_ref, ok_ref, ov_ref, of_ref):
    for n, ref in enumerate((oq_ref, ok_ref, ov_ref)):
        for i in range(NI):
            ref[i * NZ : (i + 1) * NZ, :] = r4[pl.ds(n * NI + i, NZ, stride=16), :]
    of_ref[...] = total[...]


def local(query_branch, key_branch, value_branch, query_taps, key_taps, value_taps, long_filter, grad_out):
    channels, count = query_branch.shape
    vmem = pl.BlockSpec(memory_space=pltpu.VMEM)
    hbm = pl.BlockSpec(memory_space=pltpu.HBM)
    consts = [jnp.asarray(table) for table in tables()]
    token_out = jax.ShapeDtypeStruct((channels, count), F32)
    filter_out = jax.ShapeDtypeStruct((1, count), F32)
    sems = pltpu.SemaphoreType.DMA
    rows, total = pl.pallas_call(
        kernel,
        out_shape=(jax.ShapeDtypeStruct((NZ * 16, BLK), F32), filter_out),
        in_specs=[hbm] * (8 + len(consts)),
        out_specs=(vmem,) * 2,
        scratch_shapes=[pltpu.VMEM((channels, count), BF16)] * 4
        + [pltpu.VMEM((1, count), F32)]
        + [pltpu.SMEM((3, channels), F32)] * 3
        + [pltpu.VMEM(c.shape, c.dtype) for c in consts]
        + [
            pltpu.VMEM((4 * channels, BLK), F32),
            pltpu.VMEM((NZ, 16, BLK), BF16),
            pltpu.VMEM((NZ, 16, BLK), BF16),
            pltpu.VMEM((NZ, 1, BLK), F32),
            pltpu.VMEM((NI, 4, NZ, BLK), BF16),
            pltpu.VMEM((NP, 4, NZ, BLK), BF16),
            pltpu.VMEM((NZ, BLK), F32),
            pltpu.VMEM((NP, NZ, BLK), F32),
            pltpu.VMEM((5, NB, BLK), F32),
            pltpu.VMEM((2, NB, BLK), F32),
            pltpu.VMEM((NP, 2, NZ, BLK), F32),
            pltpu.VMEM((NP, 2, NZ, BLK), F32),
            pltpu.VMEM((NZ * 16, BLK), F32),
            pltpu.VMEM((1, BLK), F32),
            pltpu.VMEM((NG, 1, BLK), F32),
            sems((8 + len(consts),)),
            sems((NZ - 1,)), sems(()), sems((NZ - 1,)), sems(()),
            sems((NP - 1,)), sems(()), sems((NP - 1,)), sems(()),
            sems((NP - 1,)), sems(()),
            sems((NZ - 1,)), sems(()),
            sems((NG - 1,)), sems(()),
        ],
        compiler_params=pltpu.CompilerParams(
            collective_id=0, has_side_effects=True, vmem_limit_bytes=56 * 1024 * 1024
        ),
    )(
        query_branch, key_branch, value_branch, grad_out, long_filter.reshape(1, count),
        query_taps.T, key_taps.T, value_taps.T, *consts,
    )
    outs = pl.pallas_call(
        unpack,
        out_shape=(token_out, token_out, token_out, filter_out),
        in_specs=[vmem] * 2,
        out_specs=(vmem,) * 4,
        compiler_params=pltpu.CompilerParams(vmem_limit_bytes=4 * 1024 * 1024),
    )(rows, total)
    return outs[0], outs[1], outs[2], outs[3].reshape(count)


def solution(mesh):
    tokens = P("grp", "ctx")
    taps = P("grp", None)
    return jax.shard_map(
        local,
        mesh=mesh,
        in_specs=(tokens, tokens, tokens, taps, taps, taps, P("ctx"), tokens),
        out_specs=(tokens, tokens, tokens, P("ctx")),
        check_vma=False,
    )
```

```python
import functools
import math

import jax
import jax.numpy as jnp
import ml_dtypes
import numpy as np
from jax import lax
from jax.experimental import pallas as pl
from jax.experimental.pallas import tpu as pltpu
from jax.sharding import PartitionSpec as P

NY, NZ, NX, NG = 2, 16, 4, 4
NP = NY * NX
NI = NP // 2
BLK = 128
NB = NY * NZ * NX
FULL = 2 * BLK * NB
MESH = pl.DeviceIdType.MESH
Z_STEPS = (8, 7, 9, 6, 10, 5, 11, 4, 12, 3, 13, 2, 14, 1, 15)
F32, BF16 = jnp.float32, jnp.bfloat16


def split_np(matrix):
    high = matrix.astype(np.float32).astype(ml_dtypes.bfloat16)
    low = (matrix - high.astype(np.float64)).astype(np.float32).astype(ml_dtypes.bfloat16)
    return np.stack([high, low])


@functools.lru_cache(maxsize=None)
def tables():
    half = np.arange(NB) + 0.5
    blocks = np.arange(NB)
    pos = np.arange(BLK)
    outer = 2.0 * np.pi * half[:, None] * blocks[None, :] / (2 * NB)
    fwd_outer = np.concatenate([np.cos(outer), -np.sin(outer)], axis=0)
    twist = 2.0 * np.pi * half[:, None] * pos[None, :] / FULL
    twists = np.stack([np.cos(twist), np.sin(twist)]).astype(np.float32)
    inner = 2.0 * np.pi * ((pos[:, None] * pos[None, :]) % BLK) / BLK
    cos, sin = np.cos(inner), np.sin(inner)
    fwd_inner = np.block([[cos, -sin], [sin, cos]])
    scale = 2.0 / (FULL * math.sqrt(BLK * NB))
    inv_outer = scale * np.concatenate([np.cos(outer).T, -np.sin(outer).T], axis=1)
    return (
        split_np(fwd_outer),
        twists,
        split_np(fwd_inner),
        split_np(fwd_inner.T.copy()),
        split_np(inv_outer),
    )


def split(value):
    high = value.astype(BF16)
    return high, (value - high.astype(F32)).astype(BF16)


def dot(left, right):
    return jnp.dot(left, right, preferred_element_type=F32)


def left_table(table, value):
    high, low = split(value)
    return dot(table[0], high) + (dot(table[0], low) + dot(table[1], high))


def right_table(value, table):
    high, low = split(value)
    return dot(high, table[0]) + (dot(low, table[0]) + dot(high, table[1]))


def earlier(value, steps):
    lane = lax.broadcasted_iota(jnp.int32, value.shape, 1)
    row = lax.broadcasted_iota(jnp.int32, value.shape, 0)
    turned = pltpu.roll(value, steps, 1)
    above = jnp.where(row == 0, 0.0, pltpu.roll(turned, 1, 0))
    return jnp.where(lane < steps, above, turned)


def later(value, steps):
    lane = lax.broadcasted_iota(jnp.int32, value.shape, 1)
    row = lax.broadcasted_iota(jnp.int32, value.shape, 0)
    turned = pltpu.roll(value, BLK - steps, 1)
    below = jnp.where(row == NB - 1, 0.0, pltpu.roll(turned, NB - 1, 0))
    return jnp.where(lane >= BLK - steps, below, turned)


def kernel(
    q_hbm, k_hbm, v_hbm, g_hbm, filt_hbm, tq_hbm, tk_hbm, tv_hbm,
    fo_hbm, tw_hbm, fi_hbm, ii_hbm, io_hbm,
    r4_hbm, of_ref,
    q_ref, k_ref, v_ref, g_ref, filt_ref, tq_ref, tk_ref, tv_ref,
    fo, tw, fi, ii, io,
    stage, s1, r1, r1f, s2, r2, s2f, r2f, tok, res, s3, r3, s4, s4f, r4f, s5, r5,
    load_sem, z_send, z_recv, zf_send, zf_recv, p_send, p_recv, pf_send, pf_recv,
    b_send, b_recv, c_send, c_recv, cf_send, cf_recv, own_sem, g_send, g_recv,
):
    me = lax.axis_index("ctx")
    grp = lax.axis_index("grp")
    y, z, x = me // (NZ * NX), (me // NX) % NZ, me % NX
    p = y * NX + x
    pair, role = p // 2, p % 2

    def z_peer(step):
        other = (z + step) % NZ
        return other, {"ctx": (y * NZ + other) * NX + x}

    def p_peer(step):
        other = (p + step) % NP
        return other, {"ctx": ((other // NX) * NZ + z) * NX + other % NX}

    def g_peer(step):
        return {"grp": (grp + step) % NG}

    loads = [
        pltpu.make_async_copy(src, dst, load_sem.at[n])
        for n, (src, dst) in enumerate(
            (
                (q_hbm, q_ref), (k_hbm, k_ref), (v_hbm, v_ref), (g_hbm, g_ref), (filt_hbm, filt_ref),
                (tq_hbm, tq_ref), (tk_hbm, tk_ref), (tv_hbm, tv_ref),
                (fo_hbm, fo), (tw_hbm, tw), (fi_hbm, fi), (ii_hbm, ii), (io_hbm, io),
            )
        )
    ]
    for load in loads[:5]:
        load.start()
    barrier = pltpu.get_barrier_semaphore()
    for step in Z_STEPS:
        pl.semaphore_signal(barrier, inc=1, device_id=z_peer(step)[1], device_id_type=MESH)
    for step in range(1, NP):
        pl.semaphore_signal(barrier, inc=1, device_id=p_peer(step)[1], device_id_type=MESH)
    for step in range(1, NG):
        pl.semaphore_signal(barrier, inc=1, device_id=g_peer(step), device_id_type=MESH)

    for load in loads[5:]:
        load.start()

    def send(src, dst, send_sem, recv_sem, target):
        copy = pltpu.make_async_remote_copy(
            src_ref=src, dst_ref=dst, send_sem=send_sem, recv_sem=recv_sem,
            device_id=target, device_id_type=MESH,
        )
        copy.start()

    def arrived(ref, sem):
        pltpu.make_async_copy(ref, ref, sem).wait()

    for load in loads[:5]:
        load.wait()
    channels = q_ref.shape[0]
    for n, ref in enumerate((q_ref, k_ref, v_ref, g_ref)):
        stage[n * channels : (n + 1) * channels, :] = ref[...].astype(F32)
    for other in range(NZ):
        s1[other] = stage[pl.ds(other, 16, stride=NZ), :].astype(BF16)
    pl.semaphore_wait(barrier, len(Z_STEPS) + NP - 1 + NG - 1)

    for step in Z_STEPS:
        other, target = z_peer(step)
        send(s1.at[other], r1.at[z], z_send, z_recv, target)
    for step in Z_STEPS:
        other, target = z_peer(step)
        send(filt_ref, r1f.at[z], zf_send, zf_recv, target)
    r1[z] = s1[z]
    r1f[z] = filt_ref[...]
    arrived(r1.at[pl.ds(0, NZ - 1)], z_recv)

    stage[...] = r1[...].astype(F32).reshape(NZ * 16, BLK)
    for i in range(NI):
        for n in range(4):
            s2[i, n] = stage[pl.ds(n * NI + i, NZ, stride=16), :].astype(BF16)
    for step in range(1, NP):
        other, target = p_peer(step)
        send(s2.at[other // 2], r2.at[p], p_send, p_recv, target)
    arrived(r1.at[pl.ds(0, NZ - 1)], z_send)
    arrived(r1f.at[pl.ds(0, NZ - 1)], zf_send)
    arrived(r1f.at[pl.ds(0, NZ - 1)], zf_recv)
    s2f[...] = r1f[...].reshape(NZ, BLK)
    for step in range(1, NP):
        other, target = p_peer(step)
        send(s2f, r2f.at[p], pf_send, pf_recv, target)
    r2[p] = s2[pair]
    r2f[p] = s2f[...]
    arrived(r2.at[pl.ds(0, NP - 1)], p_recv)

    def rows_of(other):
        return pl.ds((other // NX) * NZ * NX + other % NX, NZ, stride=NX)

    for other in range(NP):
        for n in range(4):
            tok[n, rows_of(other), :] = r2[other, n].astype(F32)
    arrived(r2f.at[pl.ds(0, NP - 1)], pf_recv)
    for other in range(NP):
        tok[4, rows_of(other), :] = r2f[other]

    channel = z + NZ * pair
    for load in loads[5:8]:
        load.wait()
    taps = [[ref[j, channel] for j in range(3)] for ref in (tq_ref, tk_ref, tv_ref)]

    def conv(value, weights):
        return weights[0] * value + weights[1] * earlier(value, 1) + weights[2] * earlier(value, 2)

    grad_out = tok[3]
    key_conv = conv(tok[1], taps[1])
    value_conv = conv(tok[2], taps[2])
    gated = key_conv * value_conv
    grad_long = grad_out * conv(tok[0], taps[0])

    for load in loads[8:]:
        load.wait()
    signals = jnp.concatenate([gated, grad_long, tok[4]], axis=1)
    outer = left_table(fo, signals)
    cos, sin = tw[0], tw[1]
    turned = []
    for n in range(3):
        re = outer[:NB, n * BLK : (n + 1) * BLK]
        im = outer[NB:, n * BLK : (n + 1) * BLK]
        turned.append(jnp.concatenate([re * cos + im * sin, im * cos - re * sin], axis=1))
    spectra = right_table(jnp.concatenate(turned, axis=0), fi)
    gated_re, gated_im = spectra[:NB, :BLK], spectra[:NB, BLK:]
    grad_re, grad_im = spectra[NB : 2 * NB, :BLK], spectra[NB : 2 * NB, BLK:]
    filt_re, filt_im = spectra[2 * NB :, :BLK], spectra[2 * NB :, BLK:]

    first = role == 0
    left_re = jnp.where(first, gated_re, grad_re)
    left_im = jnp.where(first, gated_im, grad_im)
    turn_im = jnp.where(first, filt_im, -filt_im)
    main = jnp.concatenate(
        [left_re * filt_re - left_im * turn_im, left_re * turn_im + left_im * filt_re], axis=1
    )
    cross = jnp.concatenate(
        [grad_re * gated_re + grad_im * gated_im, grad_im * gated_re - grad_re * gated_im], axis=1
    )
    inner = right_table(jnp.concatenate([main, cross], axis=0), ii)
    backs = []
    for n in range(2):
        re = inner[n * NB : (n + 1) * NB, :BLK]
        im = inner[n * NB : (n + 1) * NB, BLK:]
        backs.append(jnp.concatenate([re * cos - im * sin, im * cos + re * sin], axis=0))
    tokens = left_table(io, jnp.concatenate(backs, axis=1))
    main_tok, cross_tok = tokens[:, :BLK], tokens[:, BLK:]

    def back(value, weights):
        return weights[0] * value + weights[1] * later(value, 1) + weights[2] * later(value, 2)

    def chosen(mine, other):
        return [jnp.where(first, a, b) for a, b in zip(mine, other)]

    res[0] = back(
        main_tok * jnp.where(first, grad_out, value_conv), chosen(taps[0], taps[1])
    )
    res[1] = jnp.where(first, cross_tok, back(main_tok * key_conv, taps[2]))

    for other in range(NP):
        for n in range(2):
            s3[other, n] = res[n, rows_of(other), :]
    for step in range(1, NP):
        other, target = p_peer(step)
        send(s3.at[other], r3.at[p], b_send, b_recv, target)
    r3[p] = s3[p]
    arrived(r3.at[pl.ds(0, NP - 1)], b_recv)

    s4f[...] = ((r3[0, 1] + r3[2, 1]) + (r3[4, 1] + r3[6, 1])).reshape(NZ, 1, BLK)
    for step in Z_STEPS:
        other, target = z_peer(step)
        send(s4f.at[other], r4f.at[z], cf_send, cf_recv, target)
    for i in range(NI):
        s4[pl.ds(i, NZ, stride=16), :] = r3[2 * i, 0]
        s4[pl.ds(NI + i, NZ, stride=16), :] = r3[2 * i + 1, 0]
        s4[pl.ds(2 * NI + i, NZ, stride=16), :] = r3[2 * i + 1, 1]
    my_rows = pl.ds(pl.multiple_of(z * 16, 16), 12)
    for step in Z_STEPS:
        other, target = z_peer(step)
        rows = pl.ds(pl.multiple_of(other * 16, 16), 12)
        send(s4.at[rows], r4_hbm.at[my_rows], c_send, c_recv, target)
    own = pltpu.make_async_copy(s4.at[my_rows], r4_hbm.at[my_rows], own_sem)
    own.start()
    r4f[z] = s4f[z]
    arrived(r2.at[pl.ds(0, NP - 1)], p_send)
    arrived(r2f.at[pl.ds(0, NP - 1)], pf_send)
    arrived(r3.at[pl.ds(0, NP - 1)], b_send)
    arrived(r4f.at[pl.ds(0, NZ - 1)], cf_send)
    arrived(r4f.at[pl.ds(0, NZ - 1)], cf_recv)

    total = jnp.sum(r4f[...].reshape(NZ, BLK), axis=0, keepdims=True)
    s5[...] = total
    for step in range(1, NG):
        send(s5, r5.at[grp], g_send, g_recv, g_peer(step))
    r5[grp] = total
    own.wait()
    arrived(r5.at[pl.ds(0, NG - 1)], g_send)
    arrived(r5.at[pl.ds(0, NG - 1)], g_recv)
    of_ref[...] = (r5[0] + r5[1]) + (r5[2] + r5[3])
    arrived(s4.at[pl.ds(0, (NZ - 1) * 12)], c_send)
    arrived(s4.at[pl.ds(0, (NZ - 1) * 12)], c_recv)


def unpack(r4, total, oq_ref, ok_ref, ov_ref, of_ref, sem):
    copies = [pltpu.make_async_copy(total, of_ref, sem.at[3 * NI])]
    for n, ref in enumerate((oq_ref, ok_ref, ov_ref)):
        for i in range(NI):
            copies.append(
                pltpu.make_async_copy(
                    r4.at[:, n * NI + i, :], ref.at[pl.ds(i * NZ, NZ)], sem.at[n * NI + i]
                )
            )
    for copy in copies:
        copy.start()
    for copy in copies:
        copy.wait()


def local(query_branch, key_branch, value_branch, query_taps, key_taps, value_taps, long_filter, grad_out):
    channels, count = query_branch.shape
    vmem = pl.BlockSpec(memory_space=pltpu.VMEM)
    hbm = pl.BlockSpec(memory_space=pltpu.HBM)
    consts = [jnp.asarray(table) for table in tables()]
    token_out = jax.ShapeDtypeStruct((channels, count), F32)
    filter_out = jax.ShapeDtypeStruct((1, count), F32)
    sems = pltpu.SemaphoreType.DMA
    rows, total = pl.pallas_call(
        kernel,
        out_shape=(jax.ShapeDtypeStruct((NZ * 16, BLK), F32), filter_out),
        in_specs=[hbm] * (8 + len(consts)),
        out_specs=(hbm, vmem),
        scratch_shapes=[pltpu.VMEM((channels, count), BF16)] * 4
        + [pltpu.VMEM((1, count), F32)]
        + [pltpu.SMEM((3, channels), F32)] * 3
        + [pltpu.VMEM(c.shape, c.dtype) for c in consts]
        + [
            pltpu.VMEM((4 * channels, BLK), F32),
            pltpu.VMEM((NZ, 16, BLK), BF16),
            pltpu.VMEM((NZ, 16, BLK), BF16),
            pltpu.VMEM((NZ, 1, BLK), F32),
            pltpu.VMEM((NI, 4, NZ, BLK), BF16),
            pltpu.VMEM((NP, 4, NZ, BLK), BF16),
            pltpu.VMEM((NZ, BLK), F32),
            pltpu.VMEM((NP, NZ, BLK), F32),
            pltpu.VMEM((5, NB, BLK), F32),
            pltpu.VMEM((2, NB, BLK), F32),
            pltpu.VMEM((NP, 2, NZ, BLK), F32),
            pltpu.VMEM((NP, 2, NZ, BLK), F32),
            pltpu.VMEM((NZ * 16, BLK), F32),
            pltpu.VMEM((NZ, 1, BLK), F32),
            pltpu.VMEM((NZ, 1, BLK), F32),
            pltpu.VMEM((1, BLK), F32),
            pltpu.VMEM((NG, 1, BLK), F32),
            sems((8 + len(consts),)),
        ]
        + [sems(())] * 17,
        compiler_params=pltpu.CompilerParams(
            collective_id=0, has_side_effects=True, vmem_limit_bytes=56 * 1024 * 1024
        ),
    )(
        query_branch, key_branch, value_branch, grad_out, long_filter.reshape(1, count),
        query_taps.T, key_taps.T, value_taps.T, *consts,
    )
    outs = pl.pallas_call(
        unpack,
        out_shape=(token_out, token_out, token_out, filter_out),
        in_specs=[hbm] * 2,
        out_specs=(hbm,) * 4,
        scratch_shapes=[sems((3 * NI + 1,))],
        compiler_params=pltpu.CompilerParams(vmem_limit_bytes=56 * 1024 * 1024),
    )(rows.reshape(NZ, 16, BLK), total)
    return outs[0], outs[1], outs[2], outs[3].reshape(count)


def solution(mesh):
    tokens = P("grp", "ctx")
    taps = P("grp", None)
    return jax.shard_map(
        local,
        mesh=mesh,
        in_specs=(tokens, tokens, tokens, taps, taps, taps, P("ctx"), tokens),
        out_specs=(tokens, tokens, tokens, P("ctx")),
        check_vma=False,
    )
```

```python
import functools
import math

import jax
import jax.numpy as jnp
import ml_dtypes
import numpy as np
from jax import lax
from jax.experimental import pallas as pl
from jax.experimental.pallas import tpu as pltpu
from jax.sharding import PartitionSpec as P

NY, NZ, NX, NG = 2, 16, 4, 4
NP = NY * NX
NI = NP // 2
BLK = 128
NB = NY * NZ * NX
FULL = 2 * BLK * NB
MESH = pl.DeviceIdType.MESH
Z_STEPS = (8, 7, 9, 6, 10, 5, 11, 4, 12, 3, 13, 2, 14, 1, 15)
F32, BF16 = jnp.float32, jnp.bfloat16


def split_np(matrix):
    high = matrix.astype(np.float32).astype(ml_dtypes.bfloat16)
    low = (matrix - high.astype(np.float64)).astype(np.float32).astype(ml_dtypes.bfloat16)
    return np.stack([high, low])


@functools.lru_cache(maxsize=None)
def tables():
    half = np.arange(NB) + 0.5
    blocks = np.arange(NB)
    pos = np.arange(BLK)
    outer = 2.0 * np.pi * half[:, None] * blocks[None, :] / (2 * NB)
    fwd_outer = np.concatenate([np.cos(outer), -np.sin(outer)], axis=0)
    twist = 2.0 * np.pi * half[:, None] * pos[None, :] / FULL
    twists = np.stack([np.cos(twist), np.sin(twist)]).astype(np.float32)
    inner = 2.0 * np.pi * ((pos[:, None] * pos[None, :]) % BLK) / BLK
    cos, sin = np.cos(inner), np.sin(inner)
    fwd_inner = np.block([[cos, -sin], [sin, cos]])
    scale = 2.0 / (FULL * math.sqrt(BLK * NB))
    inv_outer = scale * np.concatenate([np.cos(outer).T, -np.sin(outer).T], axis=1)
    return (
        split_np(fwd_outer),
        twists,
        split_np(fwd_inner),
        split_np(fwd_inner.T.copy()),
        split_np(inv_outer),
    )


def split(value):
    high = value.astype(BF16)
    return high, (value - high.astype(F32)).astype(BF16)


def dot(left, right):
    return jnp.dot(left, right, preferred_element_type=F32)


def left_table(table, value):
    high, low = split(value)
    return dot(table[0], high) + (dot(table[0], low) + dot(table[1], high))


def right_table(value, table):
    high, low = split(value)
    return dot(high, table[0]) + (dot(low, table[0]) + dot(high, table[1]))


def earlier(value, steps):
    lane = lax.broadcasted_iota(jnp.int32, value.shape, 1)
    row = lax.broadcasted_iota(jnp.int32, value.shape, 0)
    turned = pltpu.roll(value, steps, 1)
    above = jnp.where(row == 0, 0.0, pltpu.roll(turned, 1, 0))
    return jnp.where(lane < steps, above, turned)


def later(value, steps):
    lane = lax.broadcasted_iota(jnp.int32, value.shape, 1)
    row = lax.broadcasted_iota(jnp.int32, value.shape, 0)
    turned = pltpu.roll(value, BLK - steps, 1)
    below = jnp.where(row == NB - 1, 0.0, pltpu.roll(turned, NB - 1, 0))
    return jnp.where(lane >= BLK - steps, below, turned)


def kernel(
    q_hbm, k_hbm, v_hbm, g_hbm, filt_hbm, tq_hbm, tk_hbm, tv_hbm,
    fo_hbm, tw_hbm, fi_hbm, ii_hbm, io_hbm,
    oq_hbm, ok_hbm, ov_hbm, of_ref,
    q_ref, k_ref, v_ref, g_ref, filt_ref, tq_ref, tk_ref, tv_ref,
    fo, tw, fi, ii, io,
    stage, s1, r1, r1f, s2, r2, s2f, r2f, tok, res, s3, r3, s4, r4, out, s4f, r4f, s5, r5,
    load_sem, z_send, z_recv, zf_send, zf_recv, p_send, p_recv, pf_send, pf_recv,
    b_send, b_recv, c_send, c_recv, cf_send, cf_recv, out_sem, g_send, g_recv,
):
    me = lax.axis_index("ctx")
    grp = lax.axis_index("grp")
    y, z, x = me // (NZ * NX), (me // NX) % NZ, me % NX
    p = y * NX + x
    pair, role = p // 2, p % 2

    def z_peer(step):
        other = (z + step) % NZ
        return other, {"ctx": (y * NZ + other) * NX + x}

    def p_peer(step):
        other = (p + step) % NP
        return other, {"ctx": ((other // NX) * NZ + z) * NX + other % NX}

    def g_peer(step):
        return {"grp": (grp + step) % NG}

    loads = [
        pltpu.make_async_copy(src, dst, load_sem.at[n])
        for n, (src, dst) in enumerate(
            (
                (q_hbm, q_ref), (k_hbm, k_ref), (v_hbm, v_ref), (g_hbm, g_ref), (filt_hbm, filt_ref),
                (tq_hbm, tq_ref), (tk_hbm, tk_ref), (tv_hbm, tv_ref),
                (fo_hbm, fo), (tw_hbm, tw), (fi_hbm, fi), (ii_hbm, ii), (io_hbm, io),
            )
        )
    ]
    for load in loads[:5]:
        load.start()
    barrier = pltpu.get_barrier_semaphore()
    for step in Z_STEPS:
        pl.semaphore_signal(barrier, inc=1, device_id=z_peer(step)[1], device_id_type=MESH)
    for step in range(1, NP):
        pl.semaphore_signal(barrier, inc=1, device_id=p_peer(step)[1], device_id_type=MESH)
    for step in range(1, NG):
        pl.semaphore_signal(barrier, inc=1, device_id=g_peer(step), device_id_type=MESH)

    for load in loads[5:]:
        load.start()

    def send(src, dst, send_sem, recv_sem, target):
        copy = pltpu.make_async_remote_copy(
            src_ref=src, dst_ref=dst, send_sem=send_sem, recv_sem=recv_sem,
            device_id=target, device_id_type=MESH,
        )
        copy.start()

    def arrived(ref, sem):
        pltpu.make_async_copy(ref, ref, sem).wait()

    for load in loads[:5]:
        load.wait()
    channels = q_ref.shape[0]
    for n, ref in enumerate((q_ref, k_ref, v_ref, g_ref)):
        stage[n * channels : (n + 1) * channels, :] = ref[...].astype(F32)
    for other in range(NZ):
        s1[other] = stage[pl.ds(other, 16, stride=NZ), :].astype(BF16)
    pl.semaphore_wait(barrier, len(Z_STEPS) + NP - 1 + NG - 1)

    for step in Z_STEPS:
        other, target = z_peer(step)
        send(s1.at[other], r1.at[z], z_send, z_recv, target)
    for step in Z_STEPS:
        other, target = z_peer(step)
        send(filt_ref, r1f.at[z], zf_send, zf_recv, target)
    r1[z] = s1[z]
    r1f[z] = filt_ref[...]
    arrived(r1.at[pl.ds(0, NZ - 1)], z_recv)

    stage[...] = r1[...].astype(F32).reshape(NZ * 16, BLK)
    for i in range(NI):
        for n in range(4):
            s2[i, n] = stage[pl.ds(n * NI + i, NZ, stride=16), :].astype(BF16)
    for step in range(1, NP):
        other, target = p_peer(step)
        send(s2.at[other // 2], r2.at[p], p_send, p_recv, target)
    arrived(r1.at[pl.ds(0, NZ - 1)], z_send)
    arrived(r1f.at[pl.ds(0, NZ - 1)], zf_send)
    arrived(r1f.at[pl.ds(0, NZ - 1)], zf_recv)
    s2f[...] = r1f[...].reshape(NZ, BLK)
    for step in range(1, NP):
        other, target = p_peer(step)
        send(s2f, r2f.at[p], pf_send, pf_recv, target)
    r2[p] = s2[pair]
    r2f[p] = s2f[...]
    arrived(r2.at[pl.ds(0, NP - 1)], p_recv)

    def rows_of(other):
        return pl.ds((other // NX) * NZ * NX + other % NX, NZ, stride=NX)

    for other in range(NP):
        for n in range(4):
            tok[n, rows_of(other), :] = r2[other, n].astype(F32)
    arrived(r2f.at[pl.ds(0, NP - 1)], pf_recv)
    for other in range(NP):
        tok[4, rows_of(other), :] = r2f[other]

    channel = z + NZ * pair
    for load in loads[5:8]:
        load.wait()
    taps = [[ref[j, channel] for j in range(3)] for ref in (tq_ref, tk_ref, tv_ref)]

    def conv(value, weights):
        return weights[0] * value + weights[1] * earlier(value, 1) + weights[2] * earlier(value, 2)

    grad_out = tok[3]
    key_conv = conv(tok[1], taps[1])
    value_conv = conv(tok[2], taps[2])
    gated = key_conv * value_conv
    grad_long = grad_out * conv(tok[0], taps[0])

    for load in loads[8:]:
        load.wait()
    signals = jnp.concatenate([gated, grad_long, tok[4]], axis=1)
    outer = left_table(fo, signals)
    cos, sin = tw[0], tw[1]
    turned = []
    for n in range(3):
        re = outer[:NB, n * BLK : (n + 1) * BLK]
        im = outer[NB:, n * BLK : (n + 1) * BLK]
        turned.append(jnp.concatenate([re * cos + im * sin, im * cos - re * sin], axis=1))
    spectra = right_table(jnp.concatenate(turned, axis=0), fi)
    gated_re, gated_im = spectra[:NB, :BLK], spectra[:NB, BLK:]
    grad_re, grad_im = spectra[NB : 2 * NB, :BLK], spectra[NB : 2 * NB, BLK:]
    filt_re, filt_im = spectra[2 * NB :, :BLK], spectra[2 * NB :, BLK:]

    first = role == 0
    left_re = jnp.where(first, gated_re, grad_re)
    left_im = jnp.where(first, gated_im, grad_im)
    turn_im = jnp.where(first, filt_im, -filt_im)
    main = jnp.concatenate(
        [left_re * filt_re - left_im * turn_im, left_re * turn_im + left_im * filt_re], axis=1
    )
    cross = jnp.concatenate(
        [grad_re * gated_re + grad_im * gated_im, grad_im * gated_re - grad_re * gated_im], axis=1
    )
    inner = right_table(jnp.concatenate([main, cross], axis=0), ii)
    backs = []
    for n in range(2):
        re = inner[n * NB : (n + 1) * NB, :BLK]
        im = inner[n * NB : (n + 1) * NB, BLK:]
        backs.append(jnp.concatenate([re * cos - im * sin, im * cos + re * sin], axis=0))
    tokens = left_table(io, jnp.concatenate(backs, axis=1))
    main_tok, cross_tok = tokens[:, :BLK], tokens[:, BLK:]

    def back(value, weights):
        return weights[0] * value + weights[1] * later(value, 1) + weights[2] * later(value, 2)

    def chosen(mine, other):
        return [jnp.where(first, a, b) for a, b in zip(mine, other)]

    res[0] = back(
        main_tok * jnp.where(first, grad_out, value_conv), chosen(taps[0], taps[1])
    )
    res[1] = jnp.where(first, cross_tok, back(main_tok * key_conv, taps[2]))

    for other in range(NP):
        for n in range(2):
            s3[other, n] = res[n, rows_of(other), :]
    for step in range(1, NP):
        other, target = p_peer(step)
        send(s3.at[other], r3.at[p], b_send, b_recv, target)
    r3[p] = s3[p]
    arrived(r3.at[pl.ds(0, NP - 1)], b_recv)

    s4f[...] = ((r3[0, 1] + r3[2, 1]) + (r3[4, 1] + r3[6, 1])).reshape(NZ, 1, BLK)
    for step in Z_STEPS:
        other, target = z_peer(step)
        send(s4f.at[other], r4f.at[z], cf_send, cf_recv, target)
    for i in range(NI):
        s4[pl.ds(i, NZ, stride=16), :] = r3[2 * i, 0]
        s4[pl.ds(NI + i, NZ, stride=16), :] = r3[2 * i + 1, 0]
        s4[pl.ds(2 * NI + i, NZ, stride=16), :] = r3[2 * i + 1, 1]
    my_rows = pl.ds(pl.multiple_of(z * 16, 16), 12)
    for step in Z_STEPS:
        other, target = z_peer(step)
        rows = pl.ds(pl.multiple_of(other * 16, 16), 12)
        send(s4.at[rows], r4.at[my_rows], c_send, c_recv, target)
    r4[my_rows, :] = s4[my_rows, :]
    r4f[z] = s4f[z]
    arrived(r2.at[pl.ds(0, NP - 1)], p_send)
    arrived(r2f.at[pl.ds(0, NP - 1)], pf_send)
    arrived(r3.at[pl.ds(0, NP - 1)], b_send)
    arrived(r4f.at[pl.ds(0, NZ - 1)], cf_send)
    arrived(r4f.at[pl.ds(0, NZ - 1)], cf_recv)

    total = jnp.sum(r4f[...].reshape(NZ, BLK), axis=0, keepdims=True)
    s5[...] = total
    for step in range(1, NG):
        send(s5, r5.at[grp], g_send, g_recv, g_peer(step))
    r5[grp] = total
    arrived(r4.at[pl.ds(0, (NZ - 1) * 12)], c_recv)
    for n in range(3):
        for i in range(NI):
            out[n, i * NZ : (i + 1) * NZ, :] = r4[pl.ds(n * NI + i, NZ, stride=16), :]
    stores = [
        pltpu.make_async_copy(out.at[n], ref, out_sem.at[n])
        for n, ref in enumerate((oq_hbm, ok_hbm, ov_hbm))
    ]
    for store in stores:
        store.start()
    arrived(s4.at[pl.ds(0, (NZ - 1) * 12)], c_send)
    arrived(r5.at[pl.ds(0, NG - 1)], g_send)
    arrived(r5.at[pl.ds(0, NG - 1)], g_recv)
    of_ref[...] = (r5[0] + r5[1]) + (r5[2] + r5[3])
    for store in stores:
        store.wait()


def passed(*refs):
    for source, target in zip(refs[:4], refs[4:]):
        target[...] = source[...]


def local(query_branch, key_branch, value_branch, query_taps, key_taps, value_taps, long_filter, grad_out):
    channels, count = query_branch.shape
    vmem = pl.BlockSpec(memory_space=pltpu.VMEM)
    hbm = pl.BlockSpec(memory_space=pltpu.HBM)
    consts = [jnp.asarray(table) for table in tables()]
    token_out = jax.ShapeDtypeStruct((channels, count), F32)
    filter_out = jax.ShapeDtypeStruct((1, count), F32)
    sems = pltpu.SemaphoreType.DMA
    made = pl.pallas_call(
        kernel,
        out_shape=(token_out, token_out, token_out, filter_out),
        in_specs=[hbm] * (8 + len(consts)),
        out_specs=(hbm, hbm, hbm, vmem),
        scratch_shapes=[pltpu.VMEM((channels, count), BF16)] * 4
        + [pltpu.VMEM((1, count), F32)]
        + [pltpu.SMEM((3, channels), F32)] * 3
        + [pltpu.VMEM(c.shape, c.dtype) for c in consts]
        + [
            pltpu.VMEM((4 * channels, BLK), F32),
            pltpu.VMEM((NZ, 16, BLK), BF16),
            pltpu.VMEM((NZ, 16, BLK), BF16),
            pltpu.VMEM((NZ, 1, BLK), F32),
            pltpu.VMEM((NI, 4, NZ, BLK), BF16),
            pltpu.VMEM((NP, 4, NZ, BLK), BF16),
            pltpu.VMEM((NZ, BLK), F32),
            pltpu.VMEM((NP, NZ, BLK), F32),
            pltpu.VMEM((5, NB, BLK), F32),
            pltpu.VMEM((2, NB, BLK), F32),
            pltpu.VMEM((NP, 2, NZ, BLK), F32),
            pltpu.VMEM((NP, 2, NZ, BLK), F32),
            pltpu.VMEM((NZ * 16, BLK), F32),
            pltpu.VMEM((NZ * 16, BLK), F32),
            pltpu.VMEM((3, channels, BLK), F32),
            pltpu.VMEM((NZ, 1, BLK), F32),
            pltpu.VMEM((NZ, 1, BLK), F32),
            pltpu.VMEM((1, BLK), F32),
            pltpu.VMEM((NG, 1, BLK), F32),
            sems((8 + len(consts),)),
        ]
        + [sems(())] * 14
        + [sems((3,)), sems(()), sems(())],
        compiler_params=pltpu.CompilerParams(
            collective_id=0, has_side_effects=True, vmem_limit_bytes=56 * 1024 * 1024
        ),
    )(
        query_branch, key_branch, value_branch, grad_out, long_filter.reshape(1, count),
        query_taps.T, key_taps.T, value_taps.T, *consts,
    )
    outs = pl.pallas_call(
        passed,
        out_shape=(token_out, token_out, token_out, filter_out),
        in_specs=[vmem] * 4,
        out_specs=(vmem,) * 4,
        compiler_params=pltpu.CompilerParams(vmem_limit_bytes=56 * 1024 * 1024),
    )(*made)
    return outs[0], outs[1], outs[2], outs[3].reshape(count)


def solution(mesh):
    tokens = P("grp", "ctx")
    taps = P("grp", None)
    return jax.shard_map(
        local,
        mesh=mesh,
        in_specs=(tokens, tokens, tokens, taps, taps, taps, P("ctx"), tokens),
        out_specs=(tokens, tokens, tokens, P("ctx")),
        check_vma=False,
    )
```

```python
import functools
import math

import jax
import jax.numpy as jnp
import ml_dtypes
import numpy as np
from jax import lax
from jax.experimental import pallas as pl
from jax.experimental.pallas import tpu as pltpu
from jax.sharding import PartitionSpec as P

NY, NZ, NX, NG = 2, 16, 4, 4
NP = NY * NX
NI = NP // 2
BLK = 128
NB = NY * NZ * NX
FULL = 2 * BLK * NB
MESH = pl.DeviceIdType.MESH
Z_STEPS = (8, 7, 9, 6, 10, 5, 11, 4, 12, 3, 13, 2, 14, 1, 15)
ZG_STEPS = [(step, turn) for step in Z_STEPS + (0,) for turn in range(NG) if step or turn]
F32, BF16 = jnp.float32, jnp.bfloat16


def split_np(matrix):
    high = matrix.astype(np.float32).astype(ml_dtypes.bfloat16)
    low = (matrix - high.astype(np.float64)).astype(np.float32).astype(ml_dtypes.bfloat16)
    return np.stack([high, low])


@functools.lru_cache(maxsize=None)
def tables():
    half = np.arange(NB) + 0.5
    blocks = np.arange(NB)
    pos = np.arange(BLK)
    outer = 2.0 * np.pi * half[:, None] * blocks[None, :] / (2 * NB)
    fwd_outer = np.concatenate([np.cos(outer), -np.sin(outer)], axis=0)
    twist = 2.0 * np.pi * half[:, None] * pos[None, :] / FULL
    twists = np.stack([np.cos(twist), np.sin(twist)]).astype(np.float32)
    inner = 2.0 * np.pi * ((pos[:, None] * pos[None, :]) % BLK) / BLK
    cos, sin = np.cos(inner), np.sin(inner)
    fwd_inner = np.block([[cos, -sin], [sin, cos]])
    scale = 2.0 / (FULL * math.sqrt(BLK * NB))
    inv_outer = scale * np.concatenate([np.cos(outer).T, -np.sin(outer).T], axis=1)
    return (
        split_np(fwd_outer),
        twists,
        split_np(fwd_inner),
        split_np(fwd_inner.T.copy()),
        split_np(inv_outer),
    )


def split(value):
    high = value.astype(BF16)
    return high, (value - high.astype(F32)).astype(BF16)


def dot(left, right):
    return jnp.dot(left, right, preferred_element_type=F32)


def left_table(table, value):
    high, low = split(value)
    return dot(table[0], high) + (dot(table[0], low) + dot(table[1], high))


def right_table(value, table):
    high, low = split(value)
    return dot(high, table[0]) + (dot(low, table[0]) + dot(high, table[1]))


def earlier(value, steps):
    lane = lax.broadcasted_iota(jnp.int32, value.shape, 1)
    row = lax.broadcasted_iota(jnp.int32, value.shape, 0)
    turned = pltpu.roll(value, steps, 1)
    above = jnp.where(row == 0, 0.0, pltpu.roll(turned, 1, 0))
    return jnp.where(lane < steps, above, turned)


def later(value, steps):
    lane = lax.broadcasted_iota(jnp.int32, value.shape, 1)
    row = lax.broadcasted_iota(jnp.int32, value.shape, 0)
    turned = pltpu.roll(value, BLK - steps, 1)
    below = jnp.where(row == NB - 1, 0.0, pltpu.roll(turned, NB - 1, 0))
    return jnp.where(lane >= BLK - steps, below, turned)


def kernel(
    q_hbm, k_hbm, v_hbm, g_hbm, filt_hbm, tq_hbm, tk_hbm, tv_hbm,
    fo_hbm, tw_hbm, fi_hbm, ii_hbm, io_hbm,
    oq_ref, ok_ref, ov_ref, of_ref,
    q_ref, k_ref, v_ref, g_ref, filt_ref, tq_ref, tk_ref, tv_ref,
    fo, tw, fi, ii, io,
    stage, s1, r1, f1, s2, r2, f2, tok, res, s3, r3, s4, r4, s4f, r4f,
    load_sem, z_send, z_recv, f1_send, f1_recv, p_send, p_recv, f2_send, f2_recv,
    b_send, b_recv, c_send, c_recv, cf_send, cf_recv,
):
    me = lax.axis_index("ctx")
    grp = lax.axis_index("grp")
    y, z, x = me // (NZ * NX), (me // NX) % NZ, me % NX
    p = y * NX + x
    pair, role = p // 2, p % 2

    def z_peer(step):
        other = (z + step) % NZ
        return other, {"ctx": (y * NZ + other) * NX + x}

    def zg_peer(step, turn):
        other, target = z_peer(step)
        return other, {**target, "grp": (grp + turn) % NG}

    def p_peer(step):
        other = (p + step) % NP
        return other, {"ctx": ((other // NX) * NZ + z) * NX + other % NX}

    loads = [
        pltpu.make_async_copy(src, dst, load_sem.at[n])
        for n, (src, dst) in enumerate(
            (
                (q_hbm, q_ref), (k_hbm, k_ref), (v_hbm, v_ref), (g_hbm, g_ref), (filt_hbm, filt_ref),
                (tq_hbm, tq_ref), (tk_hbm, tk_ref), (tv_hbm, tv_ref),
                (fo_hbm, fo), (tw_hbm, tw), (fi_hbm, fi), (ii_hbm, ii), (io_hbm, io),
            )
        )
    ]
    for load in loads[:5]:
        load.start()
    barrier = pltpu.get_barrier_semaphore()
    targets = [zg_peer(step, turn)[1] for step, turn in ZG_STEPS]
    targets += [p_peer(step)[1] for step in range(1, NP)]
    for target in targets:
        pl.semaphore_signal(barrier, inc=1, device_id=target, device_id_type=MESH)

    for load in loads[5:]:
        load.start()

    def send(src, dst, send_sem, recv_sem, target):
        copy = pltpu.make_async_remote_copy(
            src_ref=src, dst_ref=dst, send_sem=send_sem, recv_sem=recv_sem,
            device_id=target, device_id_type=MESH,
        )
        copy.start()

    def arrived(ref, sem):
        pltpu.make_async_copy(ref, ref, sem).wait()

    for load in loads[:5]:
        load.wait()
    channels = q_ref.shape[0]
    for n, ref in enumerate((q_ref, k_ref, v_ref, g_ref)):
        stage[n * channels : (n + 1) * channels, :] = ref[...].astype(F32)
    for other in range(NZ):
        s1[other] = stage[pl.ds(other, 16, stride=NZ), :].astype(BF16)
    f1[p] = filt_ref[...]
    pl.semaphore_wait(barrier, len(targets))

    for step in range(1, NP):
        send(filt_ref, f1.at[p], f1_send, f1_recv, p_peer(step)[1])

    for step in Z_STEPS:
        other, target = z_peer(step)
        send(s1.at[other], r1.at[z], z_send, z_recv, target)
    r1[z] = s1[z]
    arrived(f1.at[pl.ds(0, NP - 1)], f1_recv)
    for step in Z_STEPS:
        send(f1, f2.at[z], f2_send, f2_recv, z_peer(step)[1])
    f2[z] = f1[...]
    arrived(r1.at[pl.ds(0, NZ - 1)], z_recv)

    stage[...] = r1[...].astype(F32).reshape(NZ * 16, BLK)
    for i in range(NI):
        for n in range(4):
            s2[i, n] = stage[pl.ds(n * NI + i, NZ, stride=16), :].astype(BF16)
    for step in range(1, NP):
        other, target = p_peer(step)
        send(s2.at[other // 2], r2.at[p], p_send, p_recv, target)
    r2[p] = s2[pair]
    arrived(f1.at[pl.ds(0, NP - 1)], f1_send)
    arrived(r1.at[pl.ds(0, NZ - 1)], z_send)
    arrived(f2.at[pl.ds(0, NZ - 1)], f2_send)
    arrived(f2.at[pl.ds(0, NZ - 1)], f2_recv)
    blocks = f2[...].reshape(NB, BLK)
    for other in range(NZ):
        for n in range(NY):
            row = (other * NY + n) * NX
            to = (n * NZ + other) * NX
            tok[4, to : to + NX, :] = blocks[row : row + NX]
    for load in loads[5:]:
        load.wait()
    cos, sin = tw[0], tw[1]

    def spectra(*values):
        outer = left_table(fo, jnp.concatenate(values, axis=1))
        turned = []
        for n in range(len(values)):
            re = outer[:NB, n * BLK : (n + 1) * BLK]
            im = outer[NB:, n * BLK : (n + 1) * BLK]
            turned.append(jnp.concatenate([re * cos + im * sin, im * cos - re * sin], axis=1))
        both = right_table(jnp.concatenate(turned, axis=0), fi)
        pieces = [both[n * NB : (n + 1) * NB] for n in range(len(values))]
        return [(piece[:, :BLK], piece[:, BLK:]) for piece in pieces]

    (filt_re, filt_im), = spectra(tok[4])
    channel = z + NZ * pair
    taps = [[ref[j, channel] for j in range(3)] for ref in (tq_ref, tk_ref, tv_ref)]

    arrived(r2.at[pl.ds(0, NP - 1)], p_recv)

    def rows_of(other):
        return pl.ds((other // NX) * NZ * NX + other % NX, NZ, stride=NX)

    for other in range(NP):
        for n in range(4):
            tok[n, rows_of(other), :] = r2[other, n].astype(F32)

    def conv(value, weights):
        return weights[0] * value + weights[1] * earlier(value, 1) + weights[2] * earlier(value, 2)

    grad_out = tok[3]
    key_conv = conv(tok[1], taps[1])
    value_conv = conv(tok[2], taps[2])
    gated = key_conv * value_conv
    grad_long = grad_out * conv(tok[0], taps[0])

    (gated_re, gated_im), (grad_re, grad_im) = spectra(gated, grad_long)

    first = role == 0
    left_re = jnp.where(first, gated_re, grad_re)
    left_im = jnp.where(first, gated_im, grad_im)
    turn_im = jnp.where(first, filt_im, -filt_im)
    main = jnp.concatenate(
        [left_re * filt_re - left_im * turn_im, left_re * turn_im + left_im * filt_re], axis=1
    )
    cross = jnp.concatenate(
        [grad_re * gated_re + grad_im * gated_im, grad_im * gated_re - grad_re * gated_im], axis=1
    )
    inner = right_table(jnp.concatenate([main, cross], axis=0), ii)
    backs = []
    for n in range(2):
        re = inner[n * NB : (n + 1) * NB, :BLK]
        im = inner[n * NB : (n + 1) * NB, BLK:]
        backs.append(jnp.concatenate([re * cos - im * sin, im * cos + re * sin], axis=0))
    tokens = left_table(io, jnp.concatenate(backs, axis=1))
    main_tok, cross_tok = tokens[:, :BLK], tokens[:, BLK:]

    def back(value, weights):
        return weights[0] * value + weights[1] * later(value, 1) + weights[2] * later(value, 2)

    def chosen(mine, other):
        return [jnp.where(first, a, b) for a, b in zip(mine, other)]

    res[0] = back(
        main_tok * jnp.where(first, grad_out, value_conv), chosen(taps[0], taps[1])
    )
    res[1] = jnp.where(first, cross_tok, back(main_tok * key_conv, taps[2]))

    for other in range(NP):
        for n in range(2):
            s3[other, n] = res[n, rows_of(other), :]
    for step in range(1, NP):
        other, target = p_peer(step)
        send(s3.at[other], r3.at[p], b_send, b_recv, target)
    r3[p] = s3[p]
    arrived(r3.at[pl.ds(0, NP - 1)], b_recv)

    s4f[...] = ((r3[0, 1] + r3[2, 1]) + (r3[4, 1] + r3[6, 1])).reshape(NZ, 1, BLK)
    for step, turn in ZG_STEPS:
        other, target = zg_peer(step, turn)
        send(s4f.at[other], r4f.at[z * NG + grp], cf_send, cf_recv, target)
    for i in range(NI):
        s4[pl.ds(i, NZ, stride=16), :] = r3[2 * i, 0]
        s4[pl.ds(NI + i, NZ, stride=16), :] = r3[2 * i + 1, 0]
        s4[pl.ds(2 * NI + i, NZ, stride=16), :] = r3[2 * i + 1, 1]
    my_rows = pl.ds(pl.multiple_of(z * 16, 16), 12)
    for step in Z_STEPS:
        other, target = z_peer(step)
        rows = pl.ds(pl.multiple_of(other * 16, 16), 12)
        send(s4.at[rows], r4.at[my_rows], c_send, c_recv, target)
    r4[my_rows, :] = s4[my_rows, :]
    r4f[z * NG + grp] = s4f[z]
    arrived(r2.at[pl.ds(0, NP - 1)], p_send)
    arrived(r3.at[pl.ds(0, NP - 1)], b_send)
    arrived(r4f.at[pl.ds(0, NZ * NG - 1)], cf_send)
    arrived(r4f.at[pl.ds(0, NZ * NG - 1)], cf_recv)
    of_ref[...] = jnp.sum(r4f[...].reshape(NZ * NG, BLK), axis=0, keepdims=True)
    arrived(r4.at[pl.ds(0, (NZ - 1) * 12)], c_recv)
    for n, ref in enumerate((oq_ref, ok_ref, ov_ref)):
        for i in range(NI):
            ref[i * NZ : (i + 1) * NZ, :] = r4[pl.ds(n * NI + i, NZ, stride=16), :]
    arrived(s4.at[pl.ds(0, (NZ - 1) * 12)], c_send)


def passed(*refs):
    for source, target in zip(refs[:4], refs[4:]):
        target[...] = source[...]


def local(query_branch, key_branch, value_branch, query_taps, key_taps, value_taps, long_filter, grad_out):
    channels, count = query_branch.shape
    vmem = pl.BlockSpec(memory_space=pltpu.VMEM)
    hbm = pl.BlockSpec(memory_space=pltpu.HBM)
    consts = [jnp.asarray(table) for table in tables()]
    token_out = jax.ShapeDtypeStruct((channels, count), F32)
    filter_out = jax.ShapeDtypeStruct((1, count), F32)
    sems = pltpu.SemaphoreType.DMA
    args = [
        query_branch, key_branch, value_branch, grad_out, long_filter.reshape(1, count),
        query_taps.T, key_taps.T, value_taps.T, *consts,
    ]
    made = pl.pallas_call(
        kernel,
        out_shape=(token_out, token_out, token_out, filter_out),
        in_specs=[hbm] * (8 + len(consts)),
        out_specs=(vmem,) * 4,
        scratch_shapes=[pltpu.VMEM((channels, count), BF16)] * 4
        + [pltpu.VMEM((1, count), F32)]
        + [pltpu.SMEM((3, channels), F32)] * 3
        + [pltpu.VMEM(c.shape, c.dtype) for c in consts]
        + [
            pltpu.VMEM((4 * channels, BLK), F32),
            pltpu.VMEM((NZ, 16, BLK), BF16),
            pltpu.VMEM((NZ, 16, BLK), BF16),
            pltpu.VMEM((NP, 1, BLK), F32),
            pltpu.VMEM((NI, 4, NZ, BLK), BF16),
            pltpu.VMEM((NP, 4, NZ, BLK), BF16),
            pltpu.VMEM((NZ, NP, 1, BLK), F32),
            pltpu.VMEM((5, NB, BLK), F32),
            pltpu.VMEM((2, NB, BLK), F32),
            pltpu.VMEM((NP, 2, NZ, BLK), F32),
            pltpu.VMEM((NP, 2, NZ, BLK), F32),
            pltpu.VMEM((NZ * 16, BLK), F32),
            pltpu.VMEM((NZ * 16, BLK), F32),
            pltpu.VMEM((NZ, 1, BLK), F32),
            pltpu.VMEM((NZ * NG, 1, BLK), F32),
            sems((8 + len(consts),)),
        ]
        + [sems(())] * 14,
        compiler_params=pltpu.CompilerParams(
            collective_id=0, has_side_effects=True, vmem_limit_bytes=16 * 1024 * 1024
        ),
    )(*[pltpu.with_memory_space_constraint(arg, pltpu.HBM) for arg in args])
    outs = pl.pallas_call(
        passed,
        out_shape=(token_out, token_out, token_out, filter_out),
        in_specs=[vmem] * 4,
        out_specs=(vmem,) * 4,
        compiler_params=pltpu.CompilerParams(vmem_limit_bytes=16 * 1024 * 1024),
    )(*made)
    return outs[0], outs[1], outs[2], outs[3].reshape(count)


def solution(mesh):
    tokens = P("grp", "ctx")
    taps = P("grp", None)
    return jax.shard_map(
        local,
        mesh=mesh,
        in_specs=(tokens, tokens, tokens, taps, taps, taps, P("ctx"), tokens),
        out_specs=(tokens, tokens, tokens, P("ctx")),
        check_vma=False,
    )
```

```python
import functools
import math

import jax
import jax.numpy as jnp
import ml_dtypes
import numpy as np
from jax import lax
from jax.experimental import pallas as pl
from jax.experimental.pallas import tpu as pltpu
from jax.sharding import PartitionSpec as P

NY, NZ, NX, NG = 2, 16, 4, 4
NP = NY * NX
NI = NP // 2
BLK = 128
NB = NY * NZ * NX
FULL = 2 * BLK * NB
MESH = pl.DeviceIdType.MESH
Z_STEPS = (8, 7, 9, 6, 10, 5, 11, 4, 12, 3, 13, 2, 14, 1, 15)
QUARTER = NZ // NG
F32, BF16 = jnp.float32, jnp.bfloat16


def split_np(matrix):
    high = matrix.astype(np.float32).astype(ml_dtypes.bfloat16)
    low = (matrix - high.astype(np.float64)).astype(np.float32).astype(ml_dtypes.bfloat16)
    return np.stack([high, low])


@functools.lru_cache(maxsize=None)
def tables():
    half = np.arange(NB) + 0.5
    blocks = np.arange(NB)
    pos = np.arange(BLK)
    outer = 2.0 * np.pi * half[:, None] * blocks[None, :] / (2 * NB)
    fwd_outer = np.concatenate([np.cos(outer), -np.sin(outer)], axis=0)
    twist = 2.0 * np.pi * half[:, None] * pos[None, :] / FULL
    twists = np.stack([np.cos(twist), np.sin(twist)]).astype(np.float32)
    inner = 2.0 * np.pi * ((pos[:, None] * pos[None, :]) % BLK) / BLK
    cos, sin = np.cos(inner), np.sin(inner)
    fwd_inner = np.block([[cos, -sin], [sin, cos]])
    scale = 2.0 / (FULL * math.sqrt(BLK * NB))
    inv_outer = scale * np.concatenate([np.cos(outer).T, -np.sin(outer).T], axis=1)
    return (
        split_np(fwd_outer),
        twists,
        split_np(fwd_inner),
        split_np(fwd_inner.T.copy()),
        split_np(inv_outer),
    )


def split(value):
    high = value.astype(BF16)
    return high, (value - high.astype(F32)).astype(BF16)


def dot(left, right):
    return jnp.dot(left, right, preferred_element_type=F32)


def left_table(table, value):
    high, low = split(value)
    return dot(table[0], high) + (dot(table[0], low) + dot(table[1], high))


def right_table(value, table):
    high, low = split(value)
    return dot(high, table[0]) + (dot(low, table[0]) + dot(high, table[1]))


def earlier(value, steps):
    lane = lax.broadcasted_iota(jnp.int32, value.shape, 1)
    row = lax.broadcasted_iota(jnp.int32, value.shape, 0)
    turned = pltpu.roll(value, steps, 1)
    above = jnp.where(row == 0, 0.0, pltpu.roll(turned, 1, 0))
    return jnp.where(lane < steps, above, turned)


def later(value, steps):
    lane = lax.broadcasted_iota(jnp.int32, value.shape, 1)
    row = lax.broadcasted_iota(jnp.int32, value.shape, 0)
    turned = pltpu.roll(value, BLK - steps, 1)
    below = jnp.where(row == NB - 1, 0.0, pltpu.roll(turned, NB - 1, 0))
    return jnp.where(lane >= BLK - steps, below, turned)


def kernel(
    q_hbm, k_hbm, v_hbm, g_hbm, filt_hbm, tq_hbm, tk_hbm, tv_hbm,
    fo_hbm, tw_hbm, fi_hbm, ii_hbm, io_hbm,
    oq_ref, ok_ref, ov_ref, of_ref,
    q_ref, k_ref, v_ref, g_ref, filt_ref, tq_ref, tk_ref, tv_ref,
    fo, tw, fi, ii, io,
    stage, s1, r1, f1, s2, r2, f2, tok, res, s3, r3, s3q, r3q, s4, r4, s4f, r4f,
    load_sem, z_send, z_recv, f1_send, f1_recv, p_send, p_recv, f2_send, f2_recv,
    b_send, b_recv, q_send, q_recv, own_send, own_recv, c_send, c_recv, cf_send, cf_recv,
):
    me = lax.axis_index("ctx")
    grp = lax.axis_index("grp")
    y, z, x = me // (NZ * NX), (me // NX) % NZ, me % NX
    p = y * NX + x
    pair, role = p // 2, p % 2

    def z_peer(step):
        other = (z + step) % NZ
        return other, {"ctx": (y * NZ + other) * NX + x}

    def ctx_of(other_z, other_p):
        return ((other_p // NX) * NZ + other_z) * NX + other_p % NX

    def p_peer(step):
        other = (p + step) % NP
        return other, {"ctx": ((other // NX) * NZ + z) * NX + other % NX}

    loads = [
        pltpu.make_async_copy(src, dst, load_sem.at[n])
        for n, (src, dst) in enumerate(
            (
                (q_hbm, q_ref), (k_hbm, k_ref), (v_hbm, v_ref), (g_hbm, g_ref), (filt_hbm, filt_ref),
                (tq_hbm, tq_ref), (tk_hbm, tk_ref), (tv_hbm, tv_ref),
                (fo_hbm, fo), (tw_hbm, tw), (fi_hbm, fi), (ii_hbm, ii), (io_hbm, io),
            )
        )
    ]
    for load in loads[:5]:
        load.start()
    barrier = pltpu.get_barrier_semaphore()
    targets = [z_peer(step)[1] for step in Z_STEPS]
    targets += [p_peer(step)[1] for step in range(1, NP)]
    targets += [{"grp": (grp + turn) % NG} for turn in range(1, NG)]
    for target in targets:
        pl.semaphore_signal(barrier, inc=1, device_id=target, device_id_type=MESH)

    for load in loads[5:]:
        load.start()

    def send(src, dst, send_sem, recv_sem, target):
        copy = pltpu.make_async_remote_copy(
            src_ref=src, dst_ref=dst, send_sem=send_sem, recv_sem=recv_sem,
            device_id=target, device_id_type=MESH,
        )
        copy.start()

    def arrived(ref, sem):
        pltpu.make_async_copy(ref, ref, sem).wait()

    for load in loads[:5]:
        load.wait()
    channels = q_ref.shape[0]
    for n, ref in enumerate((q_ref, k_ref, v_ref, g_ref)):
        stage[n * channels : (n + 1) * channels, :] = ref[...].astype(F32)
    for other in range(NZ):
        s1[other] = stage[pl.ds(other, 16, stride=NZ), :].astype(BF16)
    f1[p] = filt_ref[...]
    pl.semaphore_wait(barrier, len(targets))

    for step in range(1, NP):
        send(filt_ref, f1.at[p], f1_send, f1_recv, p_peer(step)[1])

    for step in Z_STEPS:
        other, target = z_peer(step)
        send(s1.at[other], r1.at[z], z_send, z_recv, target)
    r1[z] = s1[z]
    arrived(f1.at[pl.ds(0, NP - 1)], f1_recv)
    for step in Z_STEPS:
        send(f1, f2.at[z], f2_send, f2_recv, z_peer(step)[1])
    f2[z] = f1[...]
    arrived(r1.at[pl.ds(0, NZ - 1)], z_recv)

    stage[...] = r1[...].astype(F32).reshape(NZ * 16, BLK)
    for i in range(NI):
        for n in range(4):
            s2[i, n] = stage[pl.ds(n * NI + i, NZ, stride=16), :].astype(BF16)
    for step in range(1, NP):
        other, target = p_peer(step)
        send(s2.at[other // 2], r2.at[p], p_send, p_recv, target)
    r2[p] = s2[pair]
    arrived(f1.at[pl.ds(0, NP - 1)], f1_send)
    arrived(r1.at[pl.ds(0, NZ - 1)], z_send)
    arrived(f2.at[pl.ds(0, NZ - 1)], f2_send)
    arrived(f2.at[pl.ds(0, NZ - 1)], f2_recv)
    blocks = f2[...].reshape(NB, BLK)
    for other in range(NZ):
        for n in range(NY):
            row = (other * NY + n) * NX
            to = (n * NZ + other) * NX
            tok[4, to : to + NX, :] = blocks[row : row + NX]
    for load in loads[5:]:
        load.wait()
    cos, sin = tw[0], tw[1]

    def spectra(*values):
        outer = left_table(fo, jnp.concatenate(values, axis=1))
        turned = []
        for n in range(len(values)):
            re = outer[:NB, n * BLK : (n + 1) * BLK]
            im = outer[NB:, n * BLK : (n + 1) * BLK]
            turned.append(jnp.concatenate([re * cos + im * sin, im * cos - re * sin], axis=1))
        both = right_table(jnp.concatenate(turned, axis=0), fi)
        pieces = [both[n * NB : (n + 1) * NB] for n in range(len(values))]
        return [(piece[:, :BLK], piece[:, BLK:]) for piece in pieces]

    (filt_re, filt_im), = spectra(tok[4])
    channel = z + NZ * pair
    taps = [[ref[j, channel] for j in range(3)] for ref in (tq_ref, tk_ref, tv_ref)]

    arrived(r2.at[pl.ds(0, NP - 1)], p_recv)

    def rows_of(other):
        return pl.ds((other // NX) * NZ * NX + other % NX, NZ, stride=NX)

    for other in range(NP):
        for n in range(4):
            tok[n, rows_of(other), :] = r2[other, n].astype(F32)

    def conv(value, weights):
        return weights[0] * value + weights[1] * earlier(value, 1) + weights[2] * earlier(value, 2)

    grad_out = tok[3]
    key_conv = conv(tok[1], taps[1])
    value_conv = conv(tok[2], taps[2])
    gated = key_conv * value_conv
    grad_long = grad_out * conv(tok[0], taps[0])

    (gated_re, gated_im), (grad_re, grad_im) = spectra(gated, grad_long)

    first = role == 0
    left_re = jnp.where(first, gated_re, grad_re)
    left_im = jnp.where(first, gated_im, grad_im)
    turn_im = jnp.where(first, filt_im, -filt_im)
    main = jnp.concatenate(
        [left_re * filt_re - left_im * turn_im, left_re * turn_im + left_im * filt_re], axis=1
    )
    cross = jnp.concatenate(
        [grad_re * gated_re + grad_im * gated_im, grad_im * gated_re - grad_re * gated_im], axis=1
    )
    inner = right_table(jnp.concatenate([main, cross], axis=0), ii)
    backs = []
    for n in range(2):
        re = inner[n * NB : (n + 1) * NB, :BLK]
        im = inner[n * NB : (n + 1) * NB, BLK:]
        backs.append(jnp.concatenate([re * cos - im * sin, im * cos + re * sin], axis=0))
    tokens = left_table(io, jnp.concatenate(backs, axis=1))
    main_tok, cross_tok = tokens[:, :BLK], tokens[:, BLK:]

    def back(value, weights):
        return weights[0] * value + weights[1] * later(value, 1) + weights[2] * later(value, 2)

    def chosen(mine, other):
        return [jnp.where(first, a, b) for a, b in zip(mine, other)]

    res[0] = back(
        main_tok * jnp.where(first, grad_out, value_conv), chosen(taps[0], taps[1])
    )
    res[1] = jnp.where(first, cross_tok, back(main_tok * key_conv, taps[2]))

    for other in range(NP):
        s3[other] = res[0, rows_of(other), :]
        second = res[1, rows_of(other), :]
        for part in range(NG):
            s3q[other, part] = second[part * QUARTER : (part + 1) * QUARTER]
    for step in range(1, NP):
        other, target = p_peer(step)
        send(s3.at[other], r3.at[p], b_send, b_recv, target)
        for part in range(NG):
            member = role * grp + (1 - role) * part
            slot = role * part + (1 - role) * grp
            send(
                s3q.at[other, part], r3q.at[p, slot], q_send, q_recv, {**target, "grp": member}
            )
    r3[p] = s3[p]

    @pl.when(role == 0)
    def _():
        for turn in range(1, NG):
            part = (grp + turn) % NG
            send(s3q.at[p, part], r3q.at[p, grp], own_send, own_recv, {"grp": part})
        r3q[p, grp] = s3q[p, grp]
        arrived(s3q.at[0, pl.ds(0, NG - 1)], own_send)
        arrived(s3q.at[0, pl.ds(0, NG - 1)], own_recv)

    @pl.when(role == 1)
    def _():
        r3q[p] = s3q[p]

    arrived(r3q.at[pl.ds(0, NP - 1)], q_recv)

    cross_rows = r3q[0, 0]
    for i in range(NI):
        for part in range(NG):
            if i or part:
                cross_rows = cross_rows + r3q[2 * i, part]
            s4[pl.ds(2 * NI + i + part * QUARTER * 16, QUARTER, stride=16), :] = r3q[2 * i + 1, part]
    s4f[...] = cross_rows.reshape(QUARTER, 1, BLK)
    mine = z // QUARTER == grp
    for row in range(QUARTER):
        other = grp * QUARTER + row
        for turn in range(1, NG):
            target = {"ctx": ctx_of(other, p), "grp": (grp + turn) % NG}
            send(s4f.at[row], r4f.at[z], cf_send, cf_recv, target)

        @pl.when(other != z)
        def _():
            send(s4f.at[row], r4f.at[z], cf_send, cf_recv, {"ctx": ctx_of(other, p)})

        @pl.when(other == z)
        def _():
            r4f[z] = s4f[row]

    arrived(r3.at[pl.ds(0, NP - 1)], b_recv)
    for i in range(NI):
        s4[pl.ds(i, NZ, stride=16), :] = r3[2 * i]
        s4[pl.ds(NI + i, NZ, stride=16), :] = r3[2 * i + 1]
    my_rows = pl.ds(pl.multiple_of(z * 16, 16), 12)
    for step in Z_STEPS:
        other, target = z_peer(step)
        rows = pl.ds(pl.multiple_of(other * 16, 16), 12)
        send(s4.at[rows], r4.at[my_rows], c_send, c_recv, target)
    r4[my_rows, :] = s4[my_rows, :]
    arrived(r2.at[pl.ds(0, NP - 1)], p_send)
    arrived(r3.at[pl.ds(0, NP - 1)], b_send)
    arrived(r3q.at[pl.ds(0, NP - 1)], q_send)
    for sem in (cf_send, cf_recv):

        @pl.when(mine)
        def _():
            arrived(r4f.at[pl.ds(0, NZ - 1)], sem)

        @pl.when(jnp.logical_not(mine))
        def _():
            arrived(r4f, sem)

    of_ref[...] = jnp.sum(r4f[...].reshape(NZ, BLK), axis=0, keepdims=True)
    arrived(r4.at[pl.ds(0, (NZ - 1) * 12)], c_recv)
    for n, ref in enumerate((oq_ref, ok_ref, ov_ref)):
        for i in range(NI):
            ref[i * NZ : (i + 1) * NZ, :] = r4[pl.ds(n * NI + i, NZ, stride=16), :]
    arrived(s4.at[pl.ds(0, (NZ - 1) * 12)], c_send)


def passed(*refs):
    for source, target in zip(refs[:4], refs[4:]):
        target[...] = source[...]


def local(query_branch, key_branch, value_branch, query_taps, key_taps, value_taps, long_filter, grad_out):
    channels, count = query_branch.shape
    vmem = pl.BlockSpec(memory_space=pltpu.VMEM)
    hbm = pl.BlockSpec(memory_space=pltpu.HBM)
    consts = [jnp.asarray(table) for table in tables()]
    token_out = jax.ShapeDtypeStruct((channels, count), F32)
    filter_out = jax.ShapeDtypeStruct((1, count), F32)
    sems = pltpu.SemaphoreType.DMA
    args = [
        query_branch, key_branch, value_branch, grad_out, long_filter.reshape(1, count),
        query_taps.T, key_taps.T, value_taps.T, *consts,
    ]
    made = pl.pallas_call(
        kernel,
        out_shape=(token_out, token_out, token_out, filter_out),
        in_specs=[hbm] * (8 + len(consts)),
        out_specs=(vmem,) * 4,
        scratch_shapes=[pltpu.VMEM((channels, count), BF16)] * 4
        + [pltpu.VMEM((1, count), F32)]
        + [pltpu.SMEM((3, channels), F32)] * 3
        + [pltpu.VMEM(c.shape, c.dtype) for c in consts]
        + [
            pltpu.VMEM((4 * channels, BLK), F32),
            pltpu.VMEM((NZ, 16, BLK), BF16),
            pltpu.VMEM((NZ, 16, BLK), BF16),
            pltpu.VMEM((NP, 1, BLK), F32),
            pltpu.VMEM((NI, 4, NZ, BLK), BF16),
            pltpu.VMEM((NP, 4, NZ, BLK), BF16),
            pltpu.VMEM((NZ, NP, 1, BLK), F32),
            pltpu.VMEM((5, NB, BLK), F32),
            pltpu.VMEM((2, NB, BLK), F32),
            pltpu.VMEM((NP, NZ, BLK), F32),
            pltpu.VMEM((NP, NZ, BLK), F32),
            pltpu.VMEM((NP, NG, QUARTER, BLK), F32),
            pltpu.VMEM((NP, NG, QUARTER, BLK), F32),
            pltpu.VMEM((NZ * 16, BLK), F32),
            pltpu.VMEM((NZ * 16, BLK), F32),
            pltpu.VMEM((QUARTER, 1, BLK), F32),
            pltpu.VMEM((NZ, 1, BLK), F32),
            sems((8 + len(consts),)),
        ]
        + [sems(())] * 18,
        compiler_params=pltpu.CompilerParams(
            collective_id=0, has_side_effects=True, vmem_limit_bytes=16 * 1024 * 1024
        ),
    )(*[pltpu.with_memory_space_constraint(arg, pltpu.HBM) for arg in args])
    outs = pl.pallas_call(
        passed,
        out_shape=(token_out, token_out, token_out, filter_out),
        in_specs=[vmem] * 4,
        out_specs=(vmem,) * 4,
        compiler_params=pltpu.CompilerParams(vmem_limit_bytes=16 * 1024 * 1024),
    )(*made)
    return outs[0], outs[1], outs[2], outs[3].reshape(count)


def solution(mesh):
    tokens = P("grp", "ctx")
    taps = P("grp", None)
    return jax.shard_map(
        local,
        mesh=mesh,
        in_specs=(tokens, tokens, tokens, taps, taps, taps, P("ctx"), tokens),
        out_specs=(tokens, tokens, tokens, P("ctx")),
        check_vma=False,
    )
```

```python
import functools
import math

import jax
import jax.numpy as jnp
import ml_dtypes
import numpy as np
from jax import lax
from jax.experimental import pallas as pl
from jax.experimental.pallas import tpu as pltpu
from jax.sharding import PartitionSpec as P

NY, NZ, NX, NG = 2, 16, 4, 4
NP = NY * NX
NI = NP // 2
BLK = 128
NB = NY * NZ * NX
FULL = 2 * BLK * NB
MESH = pl.DeviceIdType.MESH
Z_STEPS = (8, 7, 9, 6, 10, 5, 11, 4, 12, 3, 13, 2, 14, 1, 15)
ZG_STEPS = [(step, turn) for step in Z_STEPS + (0,) for turn in range(NG) if step or turn]
F32, BF16 = jnp.float32, jnp.bfloat16


def split_np(matrix):
    high = matrix.astype(np.float32).astype(ml_dtypes.bfloat16)
    low = (matrix - high.astype(np.float64)).astype(np.float32).astype(ml_dtypes.bfloat16)
    return np.stack([high, low])


@functools.lru_cache(maxsize=None)
def tables():
    half = np.arange(NB) + 0.5
    blocks = np.arange(NB)
    pos = np.arange(BLK)
    outer = 2.0 * np.pi * half[:, None] * blocks[None, :] / (2 * NB)
    fwd_outer = np.concatenate([np.cos(outer), -np.sin(outer)], axis=0)
    twist = 2.0 * np.pi * half[:, None] * pos[None, :] / FULL
    twists = np.stack([np.cos(twist), np.sin(twist)]).astype(np.float32)
    inner = 2.0 * np.pi * ((pos[:, None] * pos[None, :]) % BLK) / BLK
    cos, sin = np.cos(inner), np.sin(inner)
    fwd_inner = np.block([[cos, -sin], [sin, cos]])
    scale = 2.0 / (FULL * math.sqrt(BLK * NB))
    inv_outer = scale * np.concatenate([np.cos(outer).T, -np.sin(outer).T], axis=1)
    return (
        split_np(fwd_outer),
        twists,
        split_np(fwd_inner),
        split_np(fwd_inner.T.copy()),
        split_np(inv_outer),
    )


def split(value):
    high = value.astype(BF16)
    return high, (value - high.astype(F32)).astype(BF16)


def dot(left, right):
    return jnp.dot(left, right, preferred_element_type=F32)


def left_table(table, value):
    high, low = split(value)
    return dot(table[0], high) + (dot(table[0], low) + dot(table[1], high))


def right_table(value, table):
    high, low = split(value)
    return dot(high, table[0]) + (dot(low, table[0]) + dot(high, table[1]))


def earlier(value, steps):
    lane = lax.broadcasted_iota(jnp.int32, value.shape, 1)
    row = lax.broadcasted_iota(jnp.int32, value.shape, 0)
    turned = pltpu.roll(value, steps, 1)
    above = jnp.where(row == 0, 0.0, pltpu.roll(turned, 1, 0))
    return jnp.where(lane < steps, above, turned)


def later(value, steps):
    lane = lax.broadcasted_iota(jnp.int32, value.shape, 1)
    row = lax.broadcasted_iota(jnp.int32, value.shape, 0)
    turned = pltpu.roll(value, BLK - steps, 1)
    below = jnp.where(row == NB - 1, 0.0, pltpu.roll(turned, NB - 1, 0))
    return jnp.where(lane >= BLK - steps, below, turned)


def kernel(
    q_hbm, k_hbm, v_hbm, g_hbm, filt_hbm, tq_hbm, tk_hbm, tv_hbm,
    fo_hbm, tw_hbm, fi_hbm, ii_hbm, io_hbm,
    oq_ref, ok_ref, ov_ref, of_ref,
    q_ref, k_ref, v_ref, g_ref, filt_ref, tq_ref, tk_ref, tv_ref,
    fo, tw, fi, ii, io,
    stage, s1, r1, f1, s2, r2, f2, tok, res, s3, r3, s4, r4, s4f, r4f,
    load_sem, z_send, z_recv, f1_send, f1_recv, p_send, p_recv, f2_send, f2_recv,
    b_send, b_recv, c_send, c_recv, cf_send, cf_recv,
):
    me = lax.axis_index("ctx")
    grp = lax.axis_index("grp")
    y, z, x = me // (NZ * NX), (me // NX) % NZ, me % NX
    p = y * NX + x
    pair, role = p // 2, p % 2

    def z_peer(step):
        other = (z + step) % NZ
        return other, {"ctx": (y * NZ + other) * NX + x}

    def zg_peer(step, turn):
        other, target = z_peer(step)
        return other, {**target, "grp": (grp + turn) % NG}

    def p_peer(step):
        other = (p + step) % NP
        return other, {"ctx": ((other // NX) * NZ + z) * NX + other % NX}

    loads = [
        pltpu.make_async_copy(src, dst, load_sem.at[n])
        for n, (src, dst) in enumerate(
            (
                (q_hbm, q_ref), (k_hbm, k_ref), (v_hbm, v_ref), (g_hbm, g_ref), (filt_hbm, filt_ref),
                (tq_hbm, tq_ref), (tk_hbm, tk_ref), (tv_hbm, tv_ref),
                (fo_hbm, fo), (tw_hbm, tw), (fi_hbm, fi), (ii_hbm, ii), (io_hbm, io),
            )
        )
    ]
    barrier = pltpu.get_barrier_semaphore()
    targets = [z_peer(step)[1] for step in Z_STEPS]
    targets += [p_peer(step)[1] for step in range(1, NP)]
    targets += [{"grp": (grp + turn) % NG} for turn in range(1, NG)]
    for target in targets:
        pl.semaphore_signal(barrier, inc=1, device_id=target, device_id_type=MESH)

    for load in loads:
        load.start()

    def send(src, dst, send_sem, recv_sem, target):
        copy = pltpu.make_async_remote_copy(
            src_ref=src, dst_ref=dst, send_sem=send_sem, recv_sem=recv_sem,
            device_id=target, device_id_type=MESH,
        )
        copy.start()

    def arrived(ref, sem):
        pltpu.make_async_copy(ref, ref, sem).wait()

    for load in loads[:5]:
        load.wait()
    channels = q_ref.shape[0]
    for n, ref in enumerate((q_ref, k_ref, v_ref, g_ref)):
        stage[n * channels : (n + 1) * channels, :] = ref[...].astype(F32)
    for other in range(NZ):
        s1[other] = stage[pl.ds(other, 16, stride=NZ), :].astype(BF16)
    f1[p] = filt_ref[...]
    pl.semaphore_wait(barrier, len(targets))

    for step in Z_STEPS:
        other, target = z_peer(step)
        send(s1.at[other], r1.at[z], z_send, z_recv, target)
    r1[z] = s1[z]

    for step in range(1, NP):
        send(filt_ref, f1.at[p], f1_send, f1_recv, p_peer(step)[1])
    arrived(f1.at[pl.ds(0, NP - 1)], f1_recv)
    for step in Z_STEPS:
        send(f1, f2.at[z], f2_send, f2_recv, z_peer(step)[1])
    f2[z] = f1[...]
    arrived(r1.at[pl.ds(0, NZ - 1)], z_recv)

    stage[...] = r1[...].astype(F32).reshape(NZ * 16, BLK)
    for i in range(NI):
        for n in range(4):
            s2[i, n] = stage[pl.ds(n * NI + i, NZ, stride=16), :].astype(BF16)
    for step in range(1, NP):
        other, target = p_peer(step)
        send(s2.at[other // 2], r2.at[p], p_send, p_recv, target)
    r2[p] = s2[pair]
    arrived(f1.at[pl.ds(0, NP - 1)], f1_send)
    arrived(r1.at[pl.ds(0, NZ - 1)], z_send)
    arrived(f2.at[pl.ds(0, NZ - 1)], f2_send)
    arrived(f2.at[pl.ds(0, NZ - 1)], f2_recv)
    blocks = f2[...].reshape(NB, BLK)
    for other in range(NZ):
        for n in range(NY):
            row = (other * NY + n) * NX
            to = (n * NZ + other) * NX
            tok[4, to : to + NX, :] = blocks[row : row + NX]
    for load in loads[5:]:
        load.wait()
    cos, sin = tw[0], tw[1]

    def spectra(*values):
        outer = left_table(fo, jnp.concatenate(values, axis=1))
        turned = []
        for n in range(len(values)):
            re = outer[:NB, n * BLK : (n + 1) * BLK]
            im = outer[NB:, n * BLK : (n + 1) * BLK]
            turned.append(jnp.concatenate([re * cos + im * sin, im * cos - re * sin], axis=1))
        both = right_table(jnp.concatenate(turned, axis=0), fi)
        pieces = [both[n * NB : (n + 1) * NB] for n in range(len(values))]
        return [(piece[:, :BLK], piece[:, BLK:]) for piece in pieces]

    (filt_re, filt_im), = spectra(tok[4])
    channel = z + NZ * pair
    taps = [[ref[j, channel] for j in range(3)] for ref in (tq_ref, tk_ref, tv_ref)]

    arrived(r2.at[pl.ds(0, NP - 1)], p_recv)

    def rows_of(other):
        return pl.ds((other // NX) * NZ * NX + other % NX, NZ, stride=NX)

    for other in range(NP):
        for n in range(4):
            tok[n, rows_of(other), :] = r2[other, n].astype(F32)

    def conv(value, weights):
        return weights[0] * value + weights[1] * earlier(value, 1) + weights[2] * earlier(value, 2)

    grad_out = tok[3]
    key_conv = conv(tok[1], taps[1])
    value_conv = conv(tok[2], taps[2])
    gated = key_conv * value_conv
    grad_long = grad_out * conv(tok[0], taps[0])

    (gated_re, gated_im), (grad_re, grad_im) = spectra(gated, grad_long)

    first = role == 0
    left_re = jnp.where(first, gated_re, grad_re)
    left_im = jnp.where(first, gated_im, grad_im)
    turn_im = jnp.where(first, filt_im, -filt_im)
    main = jnp.concatenate(
        [left_re * filt_re - left_im * turn_im, left_re * turn_im + left_im * filt_re], axis=1
    )
    cross = jnp.concatenate(
        [grad_re * gated_re + grad_im * gated_im, grad_im * gated_re - grad_re * gated_im], axis=1
    )
    inner = right_table(jnp.concatenate([main, cross], axis=0), ii)
    backs = []
    for n in range(2):
        re = inner[n * NB : (n + 1) * NB, :BLK]
        im = inner[n * NB : (n + 1) * NB, BLK:]
        backs.append(jnp.concatenate([re * cos - im * sin, im * cos + re * sin], axis=0))
    tokens = left_table(io, jnp.concatenate(backs, axis=1))
    main_tok, cross_tok = tokens[:, :BLK], tokens[:, BLK:]

    def back(value, weights):
        return weights[0] * value + weights[1] * later(value, 1) + weights[2] * later(value, 2)

    def chosen(mine, other):
        return [jnp.where(first, a, b) for a, b in zip(mine, other)]

    res[0] = back(
        main_tok * jnp.where(first, grad_out, value_conv), chosen(taps[0], taps[1])
    )
    res[1] = jnp.where(first, cross_tok, back(main_tok * key_conv, taps[2]))

    for other in range(NP):
        for n in range(2):
            s3[other, n] = res[n, rows_of(other), :]
    for step in range(1, NP):
        other, target = p_peer(step)
        send(s3.at[other], r3.at[p], b_send, b_recv, target)
    r3[p] = s3[p]
    arrived(r3.at[pl.ds(0, NP - 1)], b_recv)

    s4f[...] = ((r3[0, 1] + r3[2, 1]) + (r3[4, 1] + r3[6, 1])).reshape(NZ, 1, BLK)
    for i in range(NI):
        s4[pl.ds(i, NZ, stride=16), :] = r3[2 * i, 0]
        s4[pl.ds(NI + i, NZ, stride=16), :] = r3[2 * i + 1, 0]
        s4[pl.ds(2 * NI + i, NZ, stride=16), :] = r3[2 * i + 1, 1]
    my_rows = pl.ds(pl.multiple_of(z * 16, 16), 12)
    for step in Z_STEPS + (0,):
        for turn in range(NG):
            other, target = zg_peer(step, turn)
            if step or turn:
                send(s4f.at[other], r4f.at[z * NG + grp], cf_send, cf_recv, target)
        if step:
            other, target = z_peer(step)
            rows = pl.ds(pl.multiple_of(other * 16, 16), 12)
            send(s4.at[rows], r4.at[my_rows], c_send, c_recv, target)
    r4[my_rows, :] = s4[my_rows, :]
    r4f[z * NG + grp] = s4f[z]
    arrived(r2.at[pl.ds(0, NP - 1)], p_send)
    arrived(r3.at[pl.ds(0, NP - 1)], b_send)
    arrived(r4f.at[pl.ds(0, NZ * NG - 1)], cf_send)
    arrived(r4f.at[pl.ds(0, NZ * NG - 1)], cf_recv)
    of_ref[...] = jnp.sum(r4f[...].reshape(NZ * NG, BLK), axis=0, keepdims=True)
    arrived(r4.at[pl.ds(0, (NZ - 1) * 12)], c_recv)
    for n, ref in enumerate((oq_ref, ok_ref, ov_ref)):
        for i in range(NI):
            ref[i * NZ : (i + 1) * NZ, :] = r4[pl.ds(n * NI + i, NZ, stride=16), :]
    arrived(s4.at[pl.ds(0, (NZ - 1) * 12)], c_send)


def passed(*refs):
    for source, target in zip(refs[:4], refs[4:]):
        target[...] = source[...]


def local(query_branch, key_branch, value_branch, query_taps, key_taps, value_taps, long_filter, grad_out):
    channels, count = query_branch.shape
    vmem = pl.BlockSpec(memory_space=pltpu.VMEM)
    hbm = pl.BlockSpec(memory_space=pltpu.HBM)
    consts = [jnp.asarray(table) for table in tables()]
    token_out = jax.ShapeDtypeStruct((channels, count), F32)
    filter_out = jax.ShapeDtypeStruct((1, count), F32)
    sems = pltpu.SemaphoreType.DMA
    args = [
        query_branch, key_branch, value_branch, grad_out, long_filter.reshape(1, count),
        query_taps.T, key_taps.T, value_taps.T, *consts,
    ]
    made = pl.pallas_call(
        kernel,
        out_shape=(token_out, token_out, token_out, filter_out),
        in_specs=[hbm] * (8 + len(consts)),
        out_specs=(vmem,) * 4,
        scratch_shapes=[pltpu.VMEM((channels, count), BF16)] * 4
        + [pltpu.VMEM((1, count), F32)]
        + [pltpu.SMEM((3, channels), F32)] * 3
        + [pltpu.VMEM(c.shape, c.dtype) for c in consts]
        + [
            pltpu.VMEM((4 * channels, BLK), F32),
            pltpu.VMEM((NZ, 16, BLK), BF16),
            pltpu.VMEM((NZ, 16, BLK), BF16),
            pltpu.VMEM((NP, 1, BLK), F32),
            pltpu.VMEM((NI, 4, NZ, BLK), BF16),
            pltpu.VMEM((NP, 4, NZ, BLK), BF16),
            pltpu.VMEM((NZ, NP, 1, BLK), F32),
            pltpu.VMEM((5, NB, BLK), F32),
            pltpu.VMEM((2, NB, BLK), F32),
            pltpu.VMEM((NP, 2, NZ, BLK), F32),
            pltpu.VMEM((NP, 2, NZ, BLK), F32),
            pltpu.VMEM((NZ * 16, BLK), F32),
            pltpu.VMEM((NZ * 16, BLK), F32),
            pltpu.VMEM((NZ, 1, BLK), F32),
            pltpu.VMEM((NZ * NG, 1, BLK), F32),
            sems((8 + len(consts),)),
        ]
        + [sems(())] * 14,
        compiler_params=pltpu.CompilerParams(
            collective_id=0, has_side_effects=True, vmem_limit_bytes=16 * 1024 * 1024
        ),
    )(*[pltpu.with_memory_space_constraint(arg, pltpu.HBM) for arg in args])
    outs = pl.pallas_call(
        passed,
        out_shape=(token_out, token_out, token_out, filter_out),
        in_specs=[vmem] * 4,
        out_specs=(vmem,) * 4,
        compiler_params=pltpu.CompilerParams(vmem_limit_bytes=16 * 1024 * 1024),
    )(*made)
    return outs[0], outs[1], outs[2], outs[3].reshape(count)


def solution(mesh):
    tokens = P("grp", "ctx")
    taps = P("grp", None)
    return jax.shard_map(
        local,
        mesh=mesh,
        in_specs=(tokens, tokens, tokens, taps, taps, taps, P("ctx"), tokens),
        out_specs=(tokens, tokens, tokens, P("ctx")),
        check_vma=False,
    )
```

```python
import functools
import math

import jax
import jax.numpy as jnp
import ml_dtypes
import numpy as np
from jax import lax
from jax.experimental import pallas as pl
from jax.experimental.pallas import tpu as pltpu
from jax.sharding import PartitionSpec as P

NY, NZ, NX, NG = 2, 16, 4, 4
NP = NY * NX
NI = NP // 2
BLK = 128
NB = NY * NZ * NX
FULL = 2 * BLK * NB
MESH = pl.DeviceIdType.MESH
Z_STEPS = (8, 7, 9, 6, 10, 5, 11, 4, 12, 3, 13, 2, 14, 1, 15)
ZG_STEPS = [(step, turn) for step in Z_STEPS + (0,) for turn in range(NG) if step or turn]
F32, BF16 = jnp.float32, jnp.bfloat16


def split_np(matrix):
    high = matrix.astype(np.float32).astype(ml_dtypes.bfloat16)
    low = (matrix - high.astype(np.float64)).astype(np.float32).astype(ml_dtypes.bfloat16)
    return np.stack([high, low])


@functools.lru_cache(maxsize=None)
def tables():
    half = np.arange(NB) + 0.5
    blocks = np.arange(NB)
    pos = np.arange(BLK)
    outer = 2.0 * np.pi * half[:, None] * blocks[None, :] / (2 * NB)
    fwd_outer = np.concatenate([np.cos(outer), -np.sin(outer)], axis=0)
    twist = 2.0 * np.pi * half[:, None] * pos[None, :] / FULL
    twists = np.stack([np.cos(twist), np.sin(twist)]).astype(np.float32)
    inner = 2.0 * np.pi * ((pos[:, None] * pos[None, :]) % BLK) / BLK
    cos, sin = np.cos(inner), np.sin(inner)
    fwd_inner = np.block([[cos, -sin], [sin, cos]])
    scale = 2.0 / (FULL * math.sqrt(BLK * NB))
    inv_outer = scale * np.concatenate([np.cos(outer).T, -np.sin(outer).T], axis=1)
    return (
        split_np(fwd_outer),
        twists,
        split_np(fwd_inner),
        split_np(fwd_inner.T.copy()),
        split_np(inv_outer),
    )


def split(value):
    high = value.astype(BF16)
    return high, (value - high.astype(F32)).astype(BF16)


def dot(left, right):
    return jnp.dot(left, right, preferred_element_type=F32)


def left_table(table, value):
    high, low = split(value)
    return dot(table[0], high) + (dot(table[0], low) + dot(table[1], high))


def right_table(value, table):
    high, low = split(value)
    return dot(high, table[0]) + (dot(low, table[0]) + dot(high, table[1]))


def earlier(value, steps):
    lane = lax.broadcasted_iota(jnp.int32, value.shape, 1)
    row = lax.broadcasted_iota(jnp.int32, value.shape, 0)
    turned = pltpu.roll(value, steps, 1)
    above = jnp.where(row == 0, 0.0, pltpu.roll(turned, 1, 0))
    return jnp.where(lane < steps, above, turned)


def later(value, steps):
    lane = lax.broadcasted_iota(jnp.int32, value.shape, 1)
    row = lax.broadcasted_iota(jnp.int32, value.shape, 0)
    turned = pltpu.roll(value, BLK - steps, 1)
    below = jnp.where(row == NB - 1, 0.0, pltpu.roll(turned, NB - 1, 0))
    return jnp.where(lane >= BLK - steps, below, turned)


def kernel(
    q_hbm, k_hbm, v_hbm, g_hbm, filt_hbm, tq_hbm, tk_hbm, tv_hbm,
    fo_hbm, tw_hbm, fi_hbm, ii_hbm, io_hbm,
    oq_ref, ok_ref, ov_ref, of_ref,
    q_ref, k_ref, v_ref, g_ref, filt_ref, tq_ref, tk_ref, tv_ref,
    fo, tw, fi, ii, io,
    stage, s1, r1, f1, s2, r2, f2, tok, res, s3, r3, s4, r4, s4f, r4f,
    load_sem, z_send, z_recv, f1_send, f1_recv, p_send, p_recv, f2_send, f2_recv,
    b_send, b_recv, d_send, d_recv, c_send, c_recv, cf_send, cf_recv,
):
    me = lax.axis_index("ctx")
    grp = lax.axis_index("grp")
    y, z, x = me // (NZ * NX), (me // NX) % NZ, me % NX
    p = y * NX + x
    pair, role = p // 2, p % 2

    def z_peer(step):
        other = (z + step) % NZ
        return other, {"ctx": (y * NZ + other) * NX + x}

    def zg_peer(step, turn):
        other, target = z_peer(step)
        return other, {**target, "grp": (grp + turn) % NG}

    def p_peer(step):
        other = (p + step) % NP
        return other, {"ctx": ((other // NX) * NZ + z) * NX + other % NX}

    loads = [
        pltpu.make_async_copy(src, dst, load_sem.at[n])
        for n, (src, dst) in enumerate(
            (
                (q_hbm, q_ref), (k_hbm, k_ref), (v_hbm, v_ref), (g_hbm, g_ref), (filt_hbm, filt_ref),
                (tq_hbm, tq_ref), (tk_hbm, tk_ref), (tv_hbm, tv_ref),
                (fo_hbm, fo), (tw_hbm, tw), (fi_hbm, fi), (ii_hbm, ii), (io_hbm, io),
            )
        )
    ]
    barrier = pltpu.get_barrier_semaphore()
    targets = [z_peer(step)[1] for step in Z_STEPS]
    targets += [p_peer(step)[1] for step in range(1, NP)]
    targets += [{"grp": (grp + turn) % NG} for turn in range(1, NG)]
    for target in targets:
        pl.semaphore_signal(barrier, inc=1, device_id=target, device_id_type=MESH)

    for load in loads:
        load.start()

    def send(src, dst, send_sem, recv_sem, target):
        copy = pltpu.make_async_remote_copy(
            src_ref=src, dst_ref=dst, send_sem=send_sem, recv_sem=recv_sem,
            device_id=target, device_id_type=MESH,
        )
        copy.start()

    def arrived(ref, sem):
        pltpu.make_async_copy(ref, ref, sem).wait()

    for load in loads[:5]:
        load.wait()
    channels = q_ref.shape[0]
    for n, ref in enumerate((q_ref, k_ref, v_ref, g_ref)):
        stage[n * channels : (n + 1) * channels, :] = ref[...].astype(F32)
    for other in range(NZ):
        s1[other] = stage[pl.ds(other, 16, stride=NZ), :].astype(BF16)
    f1[p] = filt_ref[...]
    pl.semaphore_wait(barrier, len(targets))

    for step in Z_STEPS:
        other, target = z_peer(step)
        send(s1.at[other], r1.at[z], z_send, z_recv, target)
    r1[z] = s1[z]

    for step in range(1, NP):
        send(filt_ref, f1.at[p], f1_send, f1_recv, p_peer(step)[1])
    arrived(f1.at[pl.ds(0, NP - 1)], f1_recv)
    for step in Z_STEPS:
        send(f1, f2.at[z], f2_send, f2_recv, z_peer(step)[1])
    f2[z] = f1[...]
    arrived(r1.at[pl.ds(0, NZ - 1)], z_recv)

    stage[...] = r1[...].astype(F32).reshape(NZ * 16, BLK)
    for i in range(NI):
        for n in range(4):
            s2[i, n] = stage[pl.ds(n * NI + i, NZ, stride=16), :].astype(BF16)
    for step in range(1, NP):
        other, target = p_peer(step)
        send(s2.at[other // 2], r2.at[p], p_send, p_recv, target)
    r2[p] = s2[pair]
    arrived(f1.at[pl.ds(0, NP - 1)], f1_send)
    arrived(r1.at[pl.ds(0, NZ - 1)], z_send)
    arrived(f2.at[pl.ds(0, NZ - 1)], f2_send)
    arrived(f2.at[pl.ds(0, NZ - 1)], f2_recv)
    blocks = f2[...].reshape(NB, BLK)
    for other in range(NZ):
        for n in range(NY):
            row = (other * NY + n) * NX
            to = (n * NZ + other) * NX
            tok[4, to : to + NX, :] = blocks[row : row + NX]
    for load in loads[5:]:
        load.wait()
    cos, sin = tw[0], tw[1]

    def spectra(*values):
        outer = left_table(fo, jnp.concatenate(values, axis=1))
        turned = []
        for n in range(len(values)):
            re = outer[:NB, n * BLK : (n + 1) * BLK]
            im = outer[NB:, n * BLK : (n + 1) * BLK]
            turned.append(jnp.concatenate([re * cos + im * sin, im * cos - re * sin], axis=1))
        both = right_table(jnp.concatenate(turned, axis=0), fi)
        pieces = [both[n * NB : (n + 1) * NB] for n in range(len(values))]
        return [(piece[:, :BLK], piece[:, BLK:]) for piece in pieces]

    (filt_re, filt_im), = spectra(tok[4])
    channel = z + NZ * pair
    taps = [[ref[j, channel] for j in range(3)] for ref in (tq_ref, tk_ref, tv_ref)]

    arrived(r2.at[pl.ds(0, NP - 1)], p_recv)

    def rows_of(other):
        return pl.ds((other // NX) * NZ * NX + other % NX, NZ, stride=NX)

    for other in range(NP):
        for n in range(4):
            tok[n, rows_of(other), :] = r2[other, n].astype(F32)

    def conv(value, weights):
        return weights[0] * value + weights[1] * earlier(value, 1) + weights[2] * earlier(value, 2)

    grad_out = tok[3]
    key_conv = conv(tok[1], taps[1])
    value_conv = conv(tok[2], taps[2])
    gated = key_conv * value_conv
    grad_long = grad_out * conv(tok[0], taps[0])

    (gated_re, gated_im), (grad_re, grad_im) = spectra(gated, grad_long)

    first = role == 0
    left_re = jnp.where(first, gated_re, grad_re)
    left_im = jnp.where(first, gated_im, grad_im)
    turn_im = jnp.where(first, filt_im, -filt_im)
    main = jnp.concatenate(
        [left_re * filt_re - left_im * turn_im, left_re * turn_im + left_im * filt_re], axis=1
    )
    cross = jnp.concatenate(
        [grad_re * gated_re + grad_im * gated_im, grad_im * gated_re - grad_re * gated_im], axis=1
    )
    inner = right_table(jnp.concatenate([main, cross], axis=0), ii)
    backs = []
    for n in range(2):
        re = inner[n * NB : (n + 1) * NB, :BLK]
        im = inner[n * NB : (n + 1) * NB, BLK:]
        backs.append(jnp.concatenate([re * cos - im * sin, im * cos + re * sin], axis=0))
    tokens = left_table(io, jnp.concatenate(backs, axis=1))
    main_tok, cross_tok = tokens[:, :BLK], tokens[:, BLK:]

    def back(value, weights):
        return weights[0] * value + weights[1] * later(value, 1) + weights[2] * later(value, 2)

    def chosen(mine, other):
        return [jnp.where(first, a, b) for a, b in zip(mine, other)]

    res[0] = back(
        main_tok * jnp.where(first, grad_out, value_conv), chosen(taps[0], taps[1])
    )
    res[1] = jnp.where(first, cross_tok, back(main_tok * key_conv, taps[2]))

    for other in range(NP):
        for n in range(2):
            s3[n, other] = res[n, rows_of(other), :]
    for step in range(1, NP):
        other, target = p_peer(step)
        send(s3.at[1, other], r3.at[1, p], d_send, d_recv, target)
    for step in range(1, NP):
        other, target = p_peer(step)
        send(s3.at[0, other], r3.at[0, p], b_send, b_recv, target)
    for n in range(2):
        r3[n, p] = s3[n, p]
    arrived(r3.at[1, pl.ds(0, NP - 1)], d_recv)

    s4f[...] = ((r3[1, 0] + r3[1, 2]) + (r3[1, 4] + r3[1, 6])).reshape(NZ, 1, BLK)
    for step in Z_STEPS + (0,):
        for turn in range(1 if step == 0 else 0, NG):
            other, target = zg_peer(step, turn)
            send(s4f.at[other], r4f.at[z * NG + grp], cf_send, cf_recv, target)
    arrived(r3.at[0, pl.ds(0, NP - 1)], b_recv)
    for i in range(NI):
        s4[pl.ds(i, NZ, stride=16), :] = r3[0, 2 * i]
        s4[pl.ds(NI + i, NZ, stride=16), :] = r3[0, 2 * i + 1]
        s4[pl.ds(2 * NI + i, NZ, stride=16), :] = r3[1, 2 * i + 1]
    my_rows = pl.ds(pl.multiple_of(z * 16, 16), 12)
    for step in Z_STEPS:
        other, target = z_peer(step)
        rows = pl.ds(pl.multiple_of(other * 16, 16), 12)
        send(s4.at[rows], r4.at[my_rows], c_send, c_recv, target)
    r4[my_rows, :] = s4[my_rows, :]
    r4f[z * NG + grp] = s4f[z]
    arrived(r2.at[pl.ds(0, NP - 1)], p_send)
    arrived(r3.at[0, pl.ds(0, NP - 1)], b_send)
    arrived(r3.at[0, pl.ds(0, NP - 1)], d_send)
    arrived(r4f.at[pl.ds(0, NZ * NG - 1)], cf_send)
    arrived(r4f.at[pl.ds(0, NZ * NG - 1)], cf_recv)
    of_ref[...] = jnp.sum(r4f[...].reshape(NZ * NG, BLK), axis=0, keepdims=True)
    arrived(r4.at[pl.ds(0, (NZ - 1) * 12)], c_recv)
    for n, ref in enumerate((oq_ref, ok_ref, ov_ref)):
        for i in range(NI):
            ref[i * NZ : (i + 1) * NZ, :] = r4[pl.ds(n * NI + i, NZ, stride=16), :]
    arrived(s4.at[pl.ds(0, (NZ - 1) * 12)], c_send)


def passed(*refs):
    for source, target in zip(refs[:4], refs[4:]):
        target[...] = source[...]


def local(query_branch, key_branch, value_branch, query_taps, key_taps, value_taps, long_filter, grad_out):
    channels, count = query_branch.shape
    vmem = pl.BlockSpec(memory_space=pltpu.VMEM)
    hbm = pl.BlockSpec(memory_space=pltpu.HBM)
    consts = [jnp.asarray(table) for table in tables()]
    token_out = jax.ShapeDtypeStruct((channels, count), F32)
    filter_out = jax.ShapeDtypeStruct((1, count), F32)
    sems = pltpu.SemaphoreType.DMA
    args = [
        query_branch, key_branch, value_branch, grad_out, long_filter.reshape(1, count),
        query_taps.T, key_taps.T, value_taps.T, *consts,
    ]
    made = pl.pallas_call(
        kernel,
        out_shape=(token_out, token_out, token_out, filter_out),
        in_specs=[hbm] * (8 + len(consts)),
        out_specs=(vmem,) * 4,
        scratch_shapes=[pltpu.VMEM((channels, count), BF16)] * 4
        + [pltpu.VMEM((1, count), F32)]
        + [pltpu.SMEM((3, channels), F32)] * 3
        + [pltpu.VMEM(c.shape, c.dtype) for c in consts]
        + [
            pltpu.VMEM((4 * channels, BLK), F32),
            pltpu.VMEM((NZ, 16, BLK), BF16),
            pltpu.VMEM((NZ, 16, BLK), BF16),
            pltpu.VMEM((NP, 1, BLK), F32),
            pltpu.VMEM((NI, 4, NZ, BLK), BF16),
            pltpu.VMEM((NP, 4, NZ, BLK), BF16),
            pltpu.VMEM((NZ, NP, 1, BLK), F32),
            pltpu.VMEM((5, NB, BLK), F32),
            pltpu.VMEM((2, NB, BLK), F32),
            pltpu.VMEM((2, NP, NZ, BLK), F32),
            pltpu.VMEM((2, NP, NZ, BLK), F32),
            pltpu.VMEM((NZ * 16, BLK), F32),
            pltpu.VMEM((NZ * 16, BLK), F32),
            pltpu.VMEM((NZ, 1, BLK), F32),
            pltpu.VMEM((NZ * NG, 1, BLK), F32),
            sems((8 + len(consts),)),
        ]
        + [sems(())] * 16,
        compiler_params=pltpu.CompilerParams(
            collective_id=0, has_side_effects=True, vmem_limit_bytes=16 * 1024 * 1024
        ),
    )(*[pltpu.with_memory_space_constraint(arg, pltpu.HBM) for arg in args])
    outs = pl.pallas_call(
        passed,
        out_shape=(token_out, token_out, token_out, filter_out),
        in_specs=[vmem] * 4,
        out_specs=(vmem,) * 4,
        compiler_params=pltpu.CompilerParams(vmem_limit_bytes=16 * 1024 * 1024),
    )(*made)
    return outs[0], outs[1], outs[2], outs[3].reshape(count)


def solution(mesh):
    tokens = P("grp", "ctx")
    taps = P("grp", None)
    return jax.shard_map(
        local,
        mesh=mesh,
        in_specs=(tokens, tokens, tokens, taps, taps, taps, P("ctx"), tokens),
        out_specs=(tokens, tokens, tokens, P("ctx")),
        check_vma=False,
    )
```

```python
import functools
import math

import jax
import jax.numpy as jnp
import ml_dtypes
import numpy as np
from jax import lax
from jax.experimental import pallas as pl
from jax.experimental.pallas import tpu as pltpu
from jax.sharding import PartitionSpec as P

NY, NZ, NX, NG = 2, 16, 4, 4
NP = NY * NX
NI = NP // 2
BLK = 128
NB = NY * NZ * NX
FULL = 2 * BLK * NB
MESH = pl.DeviceIdType.MESH
Z_STEPS = (8, 7, 9, 6, 10, 5, 11, 4, 12, 3, 13, 2, 14, 1, 15)
ZG_STEPS = [(step, turn) for step in Z_STEPS + (0,) for turn in range(NG) if step or turn]
F32, BF16 = jnp.float32, jnp.bfloat16


def split_np(matrix):
    high = matrix.astype(np.float32).astype(ml_dtypes.bfloat16)
    low = (matrix - high.astype(np.float64)).astype(np.float32).astype(ml_dtypes.bfloat16)
    return np.stack([high, low])


@functools.lru_cache(maxsize=None)
def tables():
    half = np.arange(NB) + 0.5
    blocks = np.arange(NB)
    pos = np.arange(BLK)
    outer = 2.0 * np.pi * half[:, None] * blocks[None, :] / (2 * NB)
    fwd_outer = np.concatenate([np.cos(outer), -np.sin(outer)], axis=0)
    twist = 2.0 * np.pi * half[:, None] * pos[None, :] / FULL
    twists = np.stack([np.cos(twist), np.sin(twist)]).astype(np.float32)
    inner = 2.0 * np.pi * ((pos[:, None] * pos[None, :]) % BLK) / BLK
    cos, sin = np.cos(inner), np.sin(inner)
    fwd_inner = np.block([[cos, -sin], [sin, cos]])
    scale = 2.0 / (FULL * math.sqrt(BLK * NB))
    inv_outer = scale * np.concatenate([np.cos(outer).T, -np.sin(outer).T], axis=1)
    return (
        split_np(fwd_outer),
        twists,
        split_np(fwd_inner),
        split_np(fwd_inner.T.copy()),
        split_np(inv_outer),
    )


def split(value):
    high = value.astype(BF16)
    return high, (value - high.astype(F32)).astype(BF16)


def dot(left, right):
    return jnp.dot(left, right, preferred_element_type=F32)


def left_table(table, value):
    high, low = split(value)
    return dot(table[0], high) + (dot(table[0], low) + dot(table[1], high))


def right_table(value, table):
    high, low = split(value)
    return dot(high, table[0]) + (dot(low, table[0]) + dot(high, table[1]))


def earlier(value, steps):
    lane = lax.broadcasted_iota(jnp.int32, value.shape, 1)
    row = lax.broadcasted_iota(jnp.int32, value.shape, 0)
    turned = pltpu.roll(value, steps, 1)
    above = jnp.where(row == 0, 0.0, pltpu.roll(turned, 1, 0))
    return jnp.where(lane < steps, above, turned)


def later(value, steps):
    lane = lax.broadcasted_iota(jnp.int32, value.shape, 1)
    row = lax.broadcasted_iota(jnp.int32, value.shape, 0)
    turned = pltpu.roll(value, BLK - steps, 1)
    below = jnp.where(row == NB - 1, 0.0, pltpu.roll(turned, NB - 1, 0))
    return jnp.where(lane >= BLK - steps, below, turned)


def kernel(
    q_hbm, k_hbm, v_hbm, g_hbm, filt_hbm, tq_hbm, tk_hbm, tv_hbm,
    fo_hbm, tw_hbm, fi_hbm, ii_hbm, io_hbm,
    oq_ref, ok_ref, ov_ref, of_ref,
    q_ref, k_ref, v_ref, g_ref, filt_ref, tq_ref, tk_ref, tv_ref,
    fo, tw, fi, ii, io,
    stage, s1, r1, f1, s2, r2, f2, tok, res, s3, r3, s4, r4, s4f, r4f,
    load_sem, z_send, z_recv, f1_send, f1_recv, p_send, p_recv, f2_send, f2_recv,
    b_send, b_recv, d_send, d_recv, c_send, c_recv, cf_send, cf_recv,
):
    me = lax.axis_index("ctx")
    grp = lax.axis_index("grp")
    y, z, x = me // (NZ * NX), (me // NX) % NZ, me % NX
    p = y * NX + x
    pair, role = p // 2, p % 2

    def z_peer(step):
        other = (z + step) % NZ
        return other, {"ctx": (y * NZ + other) * NX + x}

    def zg_peer(step, turn):
        other, target = z_peer(step)
        return other, {**target, "grp": (grp + turn) % NG}

    def p_peer(step):
        other = (p + step) % NP
        return other, {"ctx": ((other // NX) * NZ + z) * NX + other % NX}

    loads = [
        pltpu.make_async_copy(src, dst, load_sem.at[n])
        for n, (src, dst) in enumerate(
            (
                (q_hbm, q_ref), (k_hbm, k_ref), (v_hbm, v_ref), (g_hbm, g_ref), (filt_hbm, filt_ref),
                (tq_hbm, tq_ref), (tk_hbm, tk_ref), (tv_hbm, tv_ref),
                (fo_hbm, fo), (tw_hbm, tw), (fi_hbm, fi), (ii_hbm, ii), (io_hbm, io),
            )
        )
    ]
    barrier = pltpu.get_barrier_semaphore()
    targets = [z_peer(step)[1] for step in Z_STEPS]
    targets += [p_peer(step)[1] for step in range(1, NP)]
    targets += [{"grp": (grp + turn) % NG} for turn in range(1, NG)]
    for target in targets:
        pl.semaphore_signal(barrier, inc=1, device_id=target, device_id_type=MESH)

    for load in loads:
        load.start()

    def send(src, dst, send_sem, recv_sem, target):
        copy = pltpu.make_async_remote_copy(
            src_ref=src, dst_ref=dst, send_sem=send_sem, recv_sem=recv_sem,
            device_id=target, device_id_type=MESH,
        )
        copy.start()

    def arrived(ref, sem):
        pltpu.make_async_copy(ref, ref, sem).wait()

    for load in loads[:5]:
        load.wait()
    channels = q_ref.shape[0]
    for n, ref in enumerate((q_ref, k_ref, v_ref, g_ref)):
        stage[n * channels : (n + 1) * channels, :] = ref[...].astype(F32)
    for other in range(NZ):
        s1[other] = stage[pl.ds(other, 16, stride=NZ), :].astype(BF16)
    f1[p] = filt_ref[...]
    pl.semaphore_wait(barrier, len(targets))

    for step in range(1, NP):
        send(filt_ref, f1.at[p], f1_send, f1_recv, p_peer(step)[1])

    for step in Z_STEPS:
        other, target = z_peer(step)
        send(s1.at[other], r1.at[z], z_send, z_recv, target)
    r1[z] = s1[z]
    arrived(f1.at[pl.ds(0, NP - 1)], f1_recv)
    for step in Z_STEPS:
        send(f1, f2.at[z], f2_send, f2_recv, z_peer(step)[1])
    f2[z] = f1[...]
    arrived(r1.at[pl.ds(0, NZ - 1)], z_recv)

    stage[...] = r1[...].astype(F32).reshape(NZ * 16, BLK)
    for i in range(NI):
        for n in range(4):
            s2[i, n] = stage[pl.ds(n * NI + i, NZ, stride=16), :].astype(BF16)
    for step in range(1, NP):
        other, target = p_peer(step)
        send(s2.at[other // 2], r2.at[p], p_send, p_recv, target)
    r2[p] = s2[pair]
    arrived(f1.at[pl.ds(0, NP - 1)], f1_send)
    arrived(r1.at[pl.ds(0, NZ - 1)], z_send)
    arrived(f2.at[pl.ds(0, NZ - 1)], f2_send)
    arrived(f2.at[pl.ds(0, NZ - 1)], f2_recv)
    blocks = f2[...].reshape(NB, BLK)
    for other in range(NZ):
        for n in range(NY):
            row = (other * NY + n) * NX
            to = (n * NZ + other) * NX
            tok[4, to : to + NX, :] = blocks[row : row + NX]
    for load in loads[5:]:
        load.wait()
    cos, sin = tw[0], tw[1]

    def spectra(*values):
        outer = left_table(fo, jnp.concatenate(values, axis=1))
        turned = []
        for n in range(len(values)):
            re = outer[:NB, n * BLK : (n + 1) * BLK]
            im = outer[NB:, n * BLK : (n + 1) * BLK]
            turned.append(jnp.concatenate([re * cos + im * sin, im * cos - re * sin], axis=1))
        both = right_table(jnp.concatenate(turned, axis=0), fi)
        pieces = [both[n * NB : (n + 1) * NB] for n in range(len(values))]
        return [(piece[:, :BLK], piece[:, BLK:]) for piece in pieces]

    (filt_re, filt_im), = spectra(tok[4])
    channel = z + NZ * pair
    taps = [[ref[j, channel] for j in range(3)] for ref in (tq_ref, tk_ref, tv_ref)]

    arrived(r2.at[pl.ds(0, NP - 1)], p_recv)

    def rows_of(other):
        return pl.ds((other // NX) * NZ * NX + other % NX, NZ, stride=NX)

    for other in range(NP):
        for n in range(4):
            tok[n, rows_of(other), :] = r2[other, n].astype(F32)

    def conv(value, weights):
        return weights[0] * value + weights[1] * earlier(value, 1) + weights[2] * earlier(value, 2)

    grad_out = tok[3]
    key_conv = conv(tok[1], taps[1])
    value_conv = conv(tok[2], taps[2])
    gated = key_conv * value_conv
    grad_long = grad_out * conv(tok[0], taps[0])

    (gated_re, gated_im), (grad_re, grad_im) = spectra(gated, grad_long)

    first = role == 0
    left_re = jnp.where(first, gated_re, grad_re)
    left_im = jnp.where(first, gated_im, grad_im)
    turn_im = jnp.where(first, filt_im, -filt_im)
    main = jnp.concatenate(
        [left_re * filt_re - left_im * turn_im, left_re * turn_im + left_im * filt_re], axis=1
    )
    cross = jnp.concatenate(
        [grad_re * gated_re + grad_im * gated_im, grad_im * gated_re - grad_re * gated_im], axis=1
    )
    inner = right_table(jnp.concatenate([main, cross], axis=0), ii)
    backs = []
    for n in range(2):
        re = inner[n * NB : (n + 1) * NB, :BLK]
        im = inner[n * NB : (n + 1) * NB, BLK:]
        backs.append(jnp.concatenate([re * cos - im * sin, im * cos + re * sin], axis=0))
    tokens = left_table(io, jnp.concatenate(backs, axis=1))
    main_tok, cross_tok = tokens[:, :BLK], tokens[:, BLK:]

    def back(value, weights):
        return weights[0] * value + weights[1] * later(value, 1) + weights[2] * later(value, 2)

    def chosen(mine, other):
        return [jnp.where(first, a, b) for a, b in zip(mine, other)]

    res[0] = back(
        main_tok * jnp.where(first, grad_out, value_conv), chosen(taps[0], taps[1])
    )
    res[1] = jnp.where(first, cross_tok, back(main_tok * key_conv, taps[2]))

    for other in range(NP):
        for n in range(2):
            s3[n, other] = res[n, rows_of(other), :]
    for step in range(1, NP):
        other, target = p_peer(step)
        send(s3.at[1, other], r3.at[1, p], d_send, d_recv, target)
    for step in range(1, NP):
        other, target = p_peer(step)
        send(s3.at[0, other], r3.at[0, p], b_send, b_recv, target)
    for n in range(2):
        r3[n, p] = s3[n, p]
    arrived(r3.at[1, pl.ds(0, NP - 1)], d_recv)

    s4f[...] = ((r3[1, 0] + r3[1, 2]) + (r3[1, 4] + r3[1, 6])).reshape(NZ, 1, BLK)
    for step in Z_STEPS + (0,):
        for turn in range(1 if step == 0 else 0, NG):
            other, target = zg_peer(step, turn)
            send(s4f.at[other], r4f.at[z * NG + grp], cf_send, cf_recv, target)
    arrived(r3.at[0, pl.ds(0, NP - 1)], b_recv)
    for i in range(NI):
        s4[pl.ds(i, NZ, stride=16), :] = r3[0, 2 * i]
        s4[pl.ds(NI + i, NZ, stride=16), :] = r3[0, 2 * i + 1]
        s4[pl.ds(2 * NI + i, NZ, stride=16), :] = r3[1, 2 * i + 1]
    my_rows = pl.ds(pl.multiple_of(z * 16, 16), 12)
    for step in Z_STEPS:
        other, target = z_peer(step)
        rows = pl.ds(pl.multiple_of(other * 16, 16), 12)
        send(s4.at[rows], r4.at[my_rows], c_send, c_recv, target)
    r4[my_rows, :] = s4[my_rows, :]
    r4f[z * NG + grp] = s4f[z]
    arrived(r2.at[pl.ds(0, NP - 1)], p_send)
    arrived(r3.at[0, pl.ds(0, NP - 1)], b_send)
    arrived(r3.at[0, pl.ds(0, NP - 1)], d_send)
    arrived(r4f.at[pl.ds(0, NZ * NG - 1)], cf_send)
    arrived(r4f.at[pl.ds(0, NZ * NG - 1)], cf_recv)
    of_ref[...] = jnp.sum(r4f[...].reshape(NZ * NG, BLK), axis=0, keepdims=True)
    arrived(r4.at[pl.ds(0, (NZ - 1) * 12)], c_recv)
    for n, ref in enumerate((oq_ref, ok_ref, ov_ref)):
        for i in range(NI):
            ref[i * NZ : (i + 1) * NZ, :] = r4[pl.ds(n * NI + i, NZ, stride=16), :]
    arrived(s4.at[pl.ds(0, (NZ - 1) * 12)], c_send)


def passed(*refs):
    for source, target in zip(refs[:4], refs[4:]):
        target[...] = source[...]


def local(query_branch, key_branch, value_branch, query_taps, key_taps, value_taps, long_filter, grad_out):
    channels, count = query_branch.shape
    vmem = pl.BlockSpec(memory_space=pltpu.VMEM)
    hbm = pl.BlockSpec(memory_space=pltpu.HBM)
    consts = [jnp.asarray(table) for table in tables()]
    token_out = jax.ShapeDtypeStruct((channels, count), F32)
    filter_out = jax.ShapeDtypeStruct((1, count), F32)
    sems = pltpu.SemaphoreType.DMA
    args = [
        query_branch, key_branch, value_branch, grad_out, long_filter.reshape(1, count),
        query_taps.T, key_taps.T, value_taps.T, *consts,
    ]
    made = pl.pallas_call(
        kernel,
        out_shape=(token_out, token_out, token_out, filter_out),
        in_specs=[hbm] * (8 + len(consts)),
        out_specs=(vmem,) * 4,
        scratch_shapes=[pltpu.VMEM((channels, count), BF16)] * 4
        + [pltpu.VMEM((1, count), F32)]
        + [pltpu.SMEM((3, channels), F32)] * 3
        + [pltpu.VMEM(c.shape, c.dtype) for c in consts]
        + [
            pltpu.VMEM((4 * channels, BLK), F32),
            pltpu.VMEM((NZ, 16, BLK), BF16),
            pltpu.VMEM((NZ, 16, BLK), BF16),
            pltpu.VMEM((NP, 1, BLK), F32),
            pltpu.VMEM((NI, 4, NZ, BLK), BF16),
            pltpu.VMEM((NP, 4, NZ, BLK), BF16),
            pltpu.VMEM((NZ, NP, 1, BLK), F32),
            pltpu.VMEM((5, NB, BLK), F32),
            pltpu.VMEM((2, NB, BLK), F32),
            pltpu.VMEM((2, NP, NZ, BLK), F32),
            pltpu.VMEM((2, NP, NZ, BLK), F32),
            pltpu.VMEM((NZ * 16, BLK), F32),
            pltpu.VMEM((NZ * 16, BLK), F32),
            pltpu.VMEM((NZ, 1, BLK), F32),
            pltpu.VMEM((NZ * NG, 1, BLK), F32),
            sems((8 + len(consts),)),
        ]
        + [sems(())] * 16,
        compiler_params=pltpu.CompilerParams(
            collective_id=0, has_side_effects=True, vmem_limit_bytes=16 * 1024 * 1024
        ),
    )(*[pltpu.with_memory_space_constraint(arg, pltpu.HBM) for arg in args])
    outs = pl.pallas_call(
        passed,
        out_shape=(token_out, token_out, token_out, filter_out),
        in_specs=[vmem] * 4,
        out_specs=(vmem,) * 4,
        compiler_params=pltpu.CompilerParams(vmem_limit_bytes=16 * 1024 * 1024),
    )(*made)
    return outs[0], outs[1], outs[2], outs[3].reshape(count)


def solution(mesh):
    tokens = P("grp", "ctx")
    taps = P("grp", None)
    return jax.shard_map(
        local,
        mesh=mesh,
        in_specs=(tokens, tokens, tokens, taps, taps, taps, P("ctx"), tokens),
        out_specs=(tokens, tokens, tokens, P("ctx")),
        check_vma=False,
    )
```

```python
import functools
import math

import jax
import jax.numpy as jnp
import ml_dtypes
import numpy as np
from jax import lax
from jax.experimental import pallas as pl
from jax.experimental.pallas import tpu as pltpu
from jax.sharding import PartitionSpec as P

NY, NZ, NX, NG = 2, 16, 4, 4
NP = NY * NX
NI = NP // 2
BLK = 128
NB = NY * NZ * NX
FULL = 2 * BLK * NB
MESH = pl.DeviceIdType.MESH
P_STEPS = ((1, 2), (1, 1), (1, 3), (1, 0), (0, 2), (0, 1), (0, 3))
Z_STEPS = (8, 7, 9, 6, 10, 5, 11, 4, 12, 3, 13, 2, 14, 1, 15)
ZG_STEPS = [(step, turn) for step in Z_STEPS + (0,) for turn in range(NG) if step or turn]
F32, BF16 = jnp.float32, jnp.bfloat16


def split_np(matrix):
    high = matrix.astype(np.float32).astype(ml_dtypes.bfloat16)
    low = (matrix - high.astype(np.float64)).astype(np.float32).astype(ml_dtypes.bfloat16)
    return np.stack([high, low])


@functools.lru_cache(maxsize=None)
def tables():
    half = np.arange(NB) + 0.5
    blocks = np.arange(NB)
    pos = np.arange(BLK)
    outer = 2.0 * np.pi * half[:, None] * blocks[None, :] / (2 * NB)
    fwd_outer = np.concatenate([np.cos(outer), -np.sin(outer)], axis=0)
    twist = 2.0 * np.pi * half[:, None] * pos[None, :] / FULL
    twists = np.stack([np.cos(twist), np.sin(twist)]).astype(np.float32)
    inner = 2.0 * np.pi * ((pos[:, None] * pos[None, :]) % BLK) / BLK
    cos, sin = np.cos(inner), np.sin(inner)
    fwd_inner = np.block([[cos, -sin], [sin, cos]])
    scale = 2.0 / (FULL * math.sqrt(BLK * NB))
    inv_outer = scale * np.concatenate([np.cos(outer).T, -np.sin(outer).T], axis=1)
    return (
        split_np(fwd_outer),
        twists,
        split_np(fwd_inner),
        split_np(fwd_inner.T.copy()),
        split_np(inv_outer),
    )


def split(value):
    high = value.astype(BF16)
    return high, (value - high.astype(F32)).astype(BF16)


def dot(left, right):
    return jnp.dot(left, right, preferred_element_type=F32)


def left_table(table, value):
    high, low = split(value)
    return dot(table[0], high) + (dot(table[0], low) + dot(table[1], high))


def right_table(value, table):
    high, low = split(value)
    return dot(high, table[0]) + (dot(low, table[0]) + dot(high, table[1]))


def earlier(value, steps):
    lane = lax.broadcasted_iota(jnp.int32, value.shape, 1)
    row = lax.broadcasted_iota(jnp.int32, value.shape, 0)
    turned = pltpu.roll(value, steps, 1)
    above = jnp.where(row == 0, 0.0, pltpu.roll(turned, 1, 0))
    return jnp.where(lane < steps, above, turned)


def later(value, steps):
    lane = lax.broadcasted_iota(jnp.int32, value.shape, 1)
    row = lax.broadcasted_iota(jnp.int32, value.shape, 0)
    turned = pltpu.roll(value, BLK - steps, 1)
    below = jnp.where(row == NB - 1, 0.0, pltpu.roll(turned, NB - 1, 0))
    return jnp.where(lane >= BLK - steps, below, turned)


def kernel(
    q_hbm, k_hbm, v_hbm, g_hbm, filt_hbm, tq_hbm, tk_hbm, tv_hbm,
    fo_hbm, tw_hbm, fi_hbm, ii_hbm, io_hbm,
    oq_ref, ok_ref, ov_ref, of_ref,
    q_ref, k_ref, v_ref, g_ref, filt_ref, tq_ref, tk_ref, tv_ref,
    fo, tw, fi, ii, io,
    stage, s1, r1, f1, s2, r2, f2, tok, res, s3, r3, s4, r4, s4f, r4f,
    load_sem, z_send, z_recv, f1_send, f1_recv, p_send, p_recv, f2_send, f2_recv,
    b_send, b_recv, d_send, d_recv, c_send, c_recv, cf_send, cf_recv,
):
    me = lax.axis_index("ctx")
    grp = lax.axis_index("grp")
    y, z, x = me // (NZ * NX), (me // NX) % NZ, me % NX
    p = y * NX + x
    pair, role = p // 2, p % 2

    def z_peer(step):
        other = (z + step) % NZ
        return other, {"ctx": (y * NZ + other) * NX + x}

    def zg_peer(step, turn):
        other, target = z_peer(step)
        return other, {**target, "grp": (grp + turn) % NG}

    def p_peer(step):
        up, along = P_STEPS[step - 1]
        other = ((y + up) % NY) * NX + (x + along) % NX
        return other, {"ctx": ((other // NX) * NZ + z) * NX + other % NX}

    loads = [
        pltpu.make_async_copy(src, dst, load_sem.at[n])
        for n, (src, dst) in enumerate(
            (
                (q_hbm, q_ref), (k_hbm, k_ref), (v_hbm, v_ref), (g_hbm, g_ref), (filt_hbm, filt_ref),
                (tq_hbm, tq_ref), (tk_hbm, tk_ref), (tv_hbm, tv_ref),
                (fo_hbm, fo), (tw_hbm, tw), (fi_hbm, fi), (ii_hbm, ii), (io_hbm, io),
            )
        )
    ]
    barrier = pltpu.get_barrier_semaphore()
    targets = [z_peer(step)[1] for step in Z_STEPS]
    targets += [p_peer(step)[1] for step in range(1, NP)]
    targets += [{"grp": (grp + turn) % NG} for turn in range(1, NG)]
    for target in targets:
        pl.semaphore_signal(barrier, inc=1, device_id=target, device_id_type=MESH)

    for load in loads:
        load.start()

    def send(src, dst, send_sem, recv_sem, target):
        copy = pltpu.make_async_remote_copy(
            src_ref=src, dst_ref=dst, send_sem=send_sem, recv_sem=recv_sem,
            device_id=target, device_id_type=MESH,
        )
        copy.start()

    def arrived(ref, sem):
        pltpu.make_async_copy(ref, ref, sem).wait()

    for load in loads[:5]:
        load.wait()
    channels = q_ref.shape[0]
    for n, ref in enumerate((q_ref, k_ref, v_ref, g_ref)):
        stage[n * channels : (n + 1) * channels, :] = ref[...].astype(F32)
    for other in range(NZ):
        s1[other] = stage[pl.ds(other, 16, stride=NZ), :].astype(BF16)
    f1[p] = filt_ref[...]
    pl.semaphore_wait(barrier, len(targets))

    for step in range(1, NP):
        send(filt_ref, f1.at[p], f1_send, f1_recv, p_peer(step)[1])

    for step in Z_STEPS:
        other, target = z_peer(step)
        send(s1.at[other], r1.at[z], z_send, z_recv, target)
    r1[z] = s1[z]
    arrived(f1.at[pl.ds(0, NP - 1)], f1_recv)
    for step in Z_STEPS:
        send(f1, f2.at[z], f2_send, f2_recv, z_peer(step)[1])
    f2[z] = f1[...]
    arrived(r1.at[pl.ds(0, NZ - 1)], z_recv)

    stage[...] = r1[...].astype(F32).reshape(NZ * 16, BLK)
    for i in range(NI):
        for n in range(4):
            s2[i, n] = stage[pl.ds(n * NI + i, NZ, stride=16), :].astype(BF16)
    for step in range(1, NP):
        other, target = p_peer(step)
        send(s2.at[other // 2], r2.at[p], p_send, p_recv, target)
    r2[p] = s2[pair]
    arrived(f1.at[pl.ds(0, NP - 1)], f1_send)
    arrived(r1.at[pl.ds(0, NZ - 1)], z_send)
    arrived(f2.at[pl.ds(0, NZ - 1)], f2_send)
    arrived(f2.at[pl.ds(0, NZ - 1)], f2_recv)
    blocks = f2[...].reshape(NB, BLK)
    for other in range(NZ):
        for n in range(NY):
            row = (other * NY + n) * NX
            to = (n * NZ + other) * NX
            tok[4, to : to + NX, :] = blocks[row : row + NX]
    for load in loads[5:]:
        load.wait()
    cos, sin = tw[0], tw[1]

    def spectra(*values):
        outer = left_table(fo, jnp.concatenate(values, axis=1))
        turned = []
        for n in range(len(values)):
            re = outer[:NB, n * BLK : (n + 1) * BLK]
            im = outer[NB:, n * BLK : (n + 1) * BLK]
            turned.append(jnp.concatenate([re * cos + im * sin, im * cos - re * sin], axis=1))
        both = right_table(jnp.concatenate(turned, axis=0), fi)
        pieces = [both[n * NB : (n + 1) * NB] for n in range(len(values))]
        return [(piece[:, :BLK], piece[:, BLK:]) for piece in pieces]

    (filt_re, filt_im), = spectra(tok[4])
    channel = z + NZ * pair
    taps = [[ref[j, channel] for j in range(3)] for ref in (tq_ref, tk_ref, tv_ref)]

    arrived(r2.at[pl.ds(0, NP - 1)], p_recv)

    def rows_of(other):
        return pl.ds((other // NX) * NZ * NX + other % NX, NZ, stride=NX)

    for other in range(NP):
        for n in range(4):
            tok[n, rows_of(other), :] = r2[other, n].astype(F32)

    def conv(value, weights):
        return weights[0] * value + weights[1] * earlier(value, 1) + weights[2] * earlier(value, 2)

    grad_out = tok[3]
    key_conv = conv(tok[1], taps[1])
    value_conv = conv(tok[2], taps[2])
    gated = key_conv * value_conv
    grad_long = grad_out * conv(tok[0], taps[0])

    (gated_re, gated_im), (grad_re, grad_im) = spectra(gated, grad_long)

    first = role == 0
    left_re = jnp.where(first, gated_re, grad_re)
    left_im = jnp.where(first, gated_im, grad_im)
    turn_im = jnp.where(first, filt_im, -filt_im)
    main = jnp.concatenate(
        [left_re * filt_re - left_im * turn_im, left_re * turn_im + left_im * filt_re], axis=1
    )
    cross = jnp.concatenate(
        [grad_re * gated_re + grad_im * gated_im, grad_im * gated_re - grad_re * gated_im], axis=1
    )
    inner = right_table(jnp.concatenate([main, cross], axis=0), ii)
    backs = []
    for n in range(2):
        re = inner[n * NB : (n + 1) * NB, :BLK]
        im = inner[n * NB : (n + 1) * NB, BLK:]
        backs.append(jnp.concatenate([re * cos - im * sin, im * cos + re * sin], axis=0))
    tokens = left_table(io, jnp.concatenate(backs, axis=1))
    main_tok, cross_tok = tokens[:, :BLK], tokens[:, BLK:]

    def back(value, weights):
        return weights[0] * value + weights[1] * later(value, 1) + weights[2] * later(value, 2)

    def chosen(mine, other):
        return [jnp.where(first, a, b) for a, b in zip(mine, other)]

    res[0] = back(
        main_tok * jnp.where(first, grad_out, value_conv), chosen(taps[0], taps[1])
    )
    res[1] = jnp.where(first, cross_tok, back(main_tok * key_conv, taps[2]))

    for other in range(NP):
        for n in range(2):
            s3[n, other] = res[n, rows_of(other), :]
    for step in range(1, NP):
        other, target = p_peer(step)
        send(s3.at[1, other], r3.at[1, p], d_send, d_recv, target)
    for step in range(1, NP):
        other, target = p_peer(step)
        send(s3.at[0, other], r3.at[0, p], b_send, b_recv, target)
    for n in range(2):
        r3[n, p] = s3[n, p]
    arrived(r3.at[1, pl.ds(0, NP - 1)], d_recv)

    s4f[...] = ((r3[1, 0] + r3[1, 2]) + (r3[1, 4] + r3[1, 6])).reshape(NZ, 1, BLK)
    for step in Z_STEPS + (0,):
        for turn in range(1 if step == 0 else 0, NG):
            other, target = zg_peer(step, turn)
            send(s4f.at[other], r4f.at[z * NG + grp], cf_send, cf_recv, target)
    arrived(r3.at[0, pl.ds(0, NP - 1)], b_recv)
    for i in range(NI):
        s4[pl.ds(i, NZ, stride=16), :] = r3[0, 2 * i]
        s4[pl.ds(NI + i, NZ, stride=16), :] = r3[0, 2 * i + 1]
        s4[pl.ds(2 * NI + i, NZ, stride=16), :] = r3[1, 2 * i + 1]
    my_rows = pl.ds(pl.multiple_of(z * 16, 16), 12)
    for step in Z_STEPS:
        other, target = z_peer(step)
        rows = pl.ds(pl.multiple_of(other * 16, 16), 12)
        send(s4.at[rows], r4.at[my_rows], c_send, c_recv, target)
    r4[my_rows, :] = s4[my_rows, :]
    r4f[z * NG + grp] = s4f[z]
    arrived(r2.at[pl.ds(0, NP - 1)], p_send)
    arrived(r3.at[0, pl.ds(0, NP - 1)], b_send)
    arrived(r3.at[0, pl.ds(0, NP - 1)], d_send)
    arrived(r4f.at[pl.ds(0, NZ * NG - 1)], cf_send)
    arrived(r4f.at[pl.ds(0, NZ * NG - 1)], cf_recv)
    of_ref[...] = jnp.sum(r4f[...].reshape(NZ * NG, BLK), axis=0, keepdims=True)
    arrived(r4.at[pl.ds(0, (NZ - 1) * 12)], c_recv)
    for n, ref in enumerate((oq_ref, ok_ref, ov_ref)):
        for i in range(NI):
            ref[i * NZ : (i + 1) * NZ, :] = r4[pl.ds(n * NI + i, NZ, stride=16), :]
    arrived(s4.at[pl.ds(0, (NZ - 1) * 12)], c_send)


def passed(*refs):
    for source, target in zip(refs[:4], refs[4:]):
        target[...] = source[...]


def local(query_branch, key_branch, value_branch, query_taps, key_taps, value_taps, long_filter, grad_out):
    channels, count = query_branch.shape
    vmem = pl.BlockSpec(memory_space=pltpu.VMEM)
    hbm = pl.BlockSpec(memory_space=pltpu.HBM)
    consts = [jnp.asarray(table) for table in tables()]
    token_out = jax.ShapeDtypeStruct((channels, count), F32)
    filter_out = jax.ShapeDtypeStruct((1, count), F32)
    sems = pltpu.SemaphoreType.DMA
    args = [
        query_branch, key_branch, value_branch, grad_out, long_filter.reshape(1, count),
        query_taps.T, key_taps.T, value_taps.T, *consts,
    ]
    made = pl.pallas_call(
        kernel,
        out_shape=(token_out, token_out, token_out, filter_out),
        in_specs=[hbm] * (8 + len(consts)),
        out_specs=(vmem,) * 4,
        scratch_shapes=[pltpu.VMEM((channels, count), BF16)] * 4
        + [pltpu.VMEM((1, count), F32)]
        + [pltpu.SMEM((3, channels), F32)] * 3
        + [pltpu.VMEM(c.shape, c.dtype) for c in consts]
        + [
            pltpu.VMEM((4 * channels, BLK), F32),
            pltpu.VMEM((NZ, 16, BLK), BF16),
            pltpu.VMEM((NZ, 16, BLK), BF16),
            pltpu.VMEM((NP, 1, BLK), F32),
            pltpu.VMEM((NI, 4, NZ, BLK), BF16),
            pltpu.VMEM((NP, 4, NZ, BLK), BF16),
            pltpu.VMEM((NZ, NP, 1, BLK), F32),
            pltpu.VMEM((5, NB, BLK), F32),
            pltpu.VMEM((2, NB, BLK), F32),
            pltpu.VMEM((2, NP, NZ, BLK), F32),
            pltpu.VMEM((2, NP, NZ, BLK), F32),
            pltpu.VMEM((NZ * 16, BLK), F32),
            pltpu.VMEM((NZ * 16, BLK), F32),
            pltpu.VMEM((NZ, 1, BLK), F32),
            pltpu.VMEM((NZ * NG, 1, BLK), F32),
            sems((8 + len(consts),)),
        ]
        + [sems(())] * 16,
        compiler_params=pltpu.CompilerParams(
            collective_id=0, has_side_effects=True, vmem_limit_bytes=16 * 1024 * 1024
        ),
    )(*[pltpu.with_memory_space_constraint(arg, pltpu.HBM) for arg in args])
    outs = pl.pallas_call(
        passed,
        out_shape=(token_out, token_out, token_out, filter_out),
        in_specs=[vmem] * 4,
        out_specs=(vmem,) * 4,
        compiler_params=pltpu.CompilerParams(vmem_limit_bytes=16 * 1024 * 1024),
    )(*made)
    return outs[0], outs[1], outs[2], outs[3].reshape(count)


def solution(mesh):
    tokens = P("grp", "ctx")
    taps = P("grp", None)
    return jax.shard_map(
        local,
        mesh=mesh,
        in_specs=(tokens, tokens, tokens, taps, taps, taps, P("ctx"), tokens),
        out_specs=(tokens, tokens, tokens, P("ctx")),
        check_vma=False,
    )
```
